256 devices in a mesh: fsdp: 8 (over y, core), tensor: 4 (over x), replica: 8 (over z).
Axes of the slice: x: 4, y: 4, z: 8, core: 2. Of those that a mesh axis runs over, the one named last changes fastest.
Arguments:
- gradient: bfloat16 [8, 4096, 8192], P('replica', 'fsdp', 'tensor'), may hold values from -400 to 400, as said below
- momentum: float32 [8, 4096, 8192], P('replica', 'fsdp', 'tensor'), may hold values from -6 to 6
- basis: float32 [8192, 256], P('tensor', 'fsdp'), may hold values from -0.0625 to 0.0625
Outputs:
- update: bfloat16 [4096, 8192], P('fsdp', 'tensor')
- momentum_new: float32 [8, 4096, 8192], P('replica', 'fsdp', 'tensor')
- basis_new: float32 [8192, 256], P('tensor', 'fsdp')
The draws below stay inside these ranges and needn't reach their ends.
Inputs may be any that keep to these rules, and one draw needn't show every extreme that they name: gradient entries are finite real numbers.
All inputs are finite; a program needn't handle non-finite values.
Results may differ from the reference program's by a relative error of at most 0.001.
Values sent between devices are 32-bit elements; how exact they have to be, the bound alone decides.
No kernel may reach another device: no remote copies, remote signals or barrier semaphores. Data moves between devices by JAX's collectives and lax.ppermute only.
A program may use at most 64 MiB of HBM per device.

```python
import math
import jax
import jax.numpy as jnp
from jax import lax

M_ROWS = 4096
NCOLS = 8192
RANK = 256
REPL = 8


def draw_gradient(key, part):
    key_rows, key_cols, key_own = jax.random.split(key, 3)
    rows = jnp.exp(jax.random.uniform(key_rows, (1, M_ROWS, 1), jnp.float32) * math.log(10.0))
    rising = jnp.exp(jnp.arange(NCOLS, dtype=jnp.float32) / NCOLS * math.log(3.0))
    rough = jnp.exp(jax.random.uniform(key_cols, (NCOLS,), jnp.float32, -math.log(2.0), math.log(2.0)))
    cols = (rising * rough).reshape(1, 1, NCOLS)
    base = jax.random.truncated_normal(key_own, -6.0, 6.0, (REPL, M_ROWS, NCOLS), jnp.float32)
    return (base * rows * cols).astype(jnp.bfloat16)


def steps_of(rng, dims, pieces, smallest, largest):
    gain = 1.0
    for position, shards_of in pieces:
        draws = jax.random.uniform(jax.random.fold_in(jax.random.fold_in(rng, 6), position), (shards_of,), jnp.float32, smallest / len(pieces), largest / len(pieces))
        gain = gain * jnp.repeat(jnp.exp(draws), dims[position] // shards_of).reshape((-1,) + (1,) * (len(dims) - 1 - position))
    return gain


def noise(stream_key, shape, scale, most, shards=(), kind=jnp.bfloat16):
    level = steps_of(stream_key, shape, shards, -0.22, 0.18) if shards else 1.0
    array = jax.random.normal(stream_key, shape, jnp.float32) * scale * level
    return jnp.minimum(jnp.maximum(array, -most), most).astype(kind)


def setup_inputs(seed: int = 0) -> dict:
    arg_keys = jax.random.split(jax.random.key(seed), 4)
    return {
        "gradient": draw_gradient(jax.random.fold_in(arg_keys[3], 71), 0),
        "momentum": noise(arg_keys[1], (REPL, M_ROWS, NCOLS), 1.0, 6.0, ((0, 8), (1, 8), (2, 4)), jnp.float32),
        "basis": noise(arg_keys[2], (NCOLS, RANK), NCOLS ** -0.5, 0.0625, ((0, 4), (1, 8)), jnp.float32),
    }


HIGH = lax.Precision.HIGHEST

def reference(gradient, momentum, basis):
    count = gradient.shape[0]

    def left_term(index):
        buffer = momentum[index] + gradient[index].astype(jnp.float32)
        return jnp.dot(buffer.astype(jnp.float32), basis.astype(jnp.float32), precision=HIGH, preferred_element_type=jnp.float32)
    left = lax.optimization_barrier(jnp.sum(lax.map(left_term, jnp.arange(count)), axis=0)) / count
    gram = jnp.dot(left.T.astype(jnp.float32), left.astype(jnp.float32), precision=HIGH, preferred_element_type=jnp.float32)
    chol = jnp.linalg.cholesky(gram)
    ortho = lax.linalg.triangular_solve(chol, left, left_side=False, lower=True, transpose_a=True)

    def right_term(index):
        buffer = momentum[index] + gradient[index].astype(jnp.float32)
        return jnp.dot(buffer.T.astype(jnp.float32), ortho.astype(jnp.float32), precision=HIGH, preferred_element_type=jnp.float32)
    right = lax.optimization_barrier(jnp.sum(lax.map(right_term, jnp.arange(count)), axis=0)) / count
    norms = jnp.sqrt(lax.optimization_barrier(jnp.sum(right * right, axis=0)) + 1e-12)
    basis_new = right / norms
    lowrank = jnp.dot(ortho.astype(jnp.float32), right.T.astype(jnp.float32), precision=HIGH, preferred_element_type=jnp.float32)

    def feedback(index):
        buffer = momentum[index] + gradient[index].astype(jnp.float32)
        return buffer - 0.05 * lowrank
    momentum_new = lax.map(feedback, jnp.arange(count))
    scale = (M_ROWS * NCOLS / RANK) ** 0.5
    update = (scale * jnp.dot(ortho.astype(jnp.float32), basis_new.T.astype(jnp.float32), precision=HIGH, preferred_element_type=jnp.float32)).astype(jnp.bfloat16)
    return (update, momentum_new, basis_new)
```

```python
import functools
import jax, jax.numpy as jnp
from jax import lax
from jax.experimental import pallas as pl
from jax.experimental.pallas import tpu as pltpu
from jax.sharding import Mesh
from jax.sharding import PartitionSpec as P

M_ROWS = 4096
NCOLS = 8192
HIGH = lax.Precision.HIGHEST
RANK = 256
LEAF = 64

def leaf_inverse(block):
    side = block.shape[0]
    groups = side // 8
    lane = lax.broadcasted_iota(jnp.int32, (side, side), 1)
    line = lax.broadcasted_iota(jnp.int32, (side, side), 0)
    unit = jnp.where(lane == line, 1.0, 0.0).astype(jnp.float32)
    both = jnp.concatenate([block, unit], axis=1)
    tiles = [both[8 * g : 8 * g + 8] for g in range(groups)]
    width = 2 * side
    sub = lax.broadcasted_iota(jnp.int32, (8, width), 0)
    scales = [jnp.zeros((8, width), jnp.float32) for _ in range(groups)]
    for k in range(side):
        own, at = divmod(k, 8)
        row = jnp.broadcast_to(tiles[own][at : at + 1], (8, width))
        pivot = jnp.broadcast_to(row[:, k : k + 1], (8, width))
        scales[own] = jnp.where(sub == at, pivot, scales[own])
        if k == side - 1:
            break
        scaled = row / pivot
        for g in range(own, groups):
            if g == own and at == 7:
                continue
            column = jnp.broadcast_to(tiles[g][:, k : k + 1], (8, width))
            if g == own:
                column = jnp.where(sub > at, column, 0.0)
            tiles[g] = tiles[g] - column * scaled
    full = jnp.concatenate([t[:, side:] * lax.rsqrt(s)[:, side:] for t, s in zip(tiles, scales)], axis=0)
    return full

def factor_kernel(first, last, gram_ref, inv_ref, gram_out, inv_out):
    gram_out[...] = gram_ref[...]
    inv_out[...] = inv_ref[...]
    for i in range(first, last):
        lo, hi = i * LEAF, (i + 1) * LEAF
        leaf = leaf_inverse(gram_out[lo:hi, lo:hi])
        rows_g = jnp.dot(leaf, gram_out[lo:hi, :], precision=HIGH, preferred_element_type=jnp.float32)
        rows_i = jnp.dot(leaf, inv_out[lo:hi, :], precision=HIGH, preferred_element_type=jnp.float32)
        inv_out[lo:hi, :] = rows_i
        if hi < RANK:
            cols = rows_g[:, hi:] if hi % 128 == 0 else rows_g[:, hi - 64:]
            tall = cols.T
            if hi % 128: tall = tall[64:]
            gram_out[hi:, :] = gram_out[hi:, :] - jnp.dot(tall, rows_g, precision=HIGH, preferred_element_type=jnp.float32)
            inv_out[hi:, :] = inv_out[hi:, :] - jnp.dot(tall, rows_i, precision=HIGH, preferred_element_type=jnp.float32)

def factor_part(gram, inv, first, last):
    shape = jax.ShapeDtypeStruct((RANK, RANK), jnp.float32)
    return pl.pallas_call(
        functools.partial(factor_kernel, first, last),
        out_shape=(shape, shape),
        compiler_params=pltpu.CompilerParams(vmem_limit_bytes=16 << 20),
        cost_estimate=pl.CostEstimate(flops=0, bytes_accessed=(last-first)*15_000_000, transcendentals=0),
    )(gram, inv)


def to_everyone(value, axis):
    size = lax.axis_size(axis)
    return lax.all_to_all(
        jnp.broadcast_to(value[None], (size, *value.shape)), axis, 0, 0, tiled=True
    )


def stacked(value, axis):
    blocks = to_everyone(value, axis)
    return blocks.reshape(blocks.shape[0] * blocks.shape[1], *blocks.shape[2:])


def scattered_sum(value, axis):
    size = lax.axis_size(axis)
    blocks = value.reshape(size, value.shape[0] // size, *value.shape[1:])
    return lax.all_to_all(blocks, axis, 0, 0, tiled=True).sum(axis=0)


def swapped(value):
    return lax.ppermute(value, "core", [(0, 1), (1, 0)])


def core_scattered(value):
    half = value.shape[0] // 2
    core = lax.axis_index("core")
    sent = lax.dynamic_slice_in_dim(value, (1 - core) * half, half, 0)
    kept = lax.dynamic_slice_in_dim(value, core * half, half, 0)
    return kept + swapped(sent)


def core_joined(value):
    other = swapped(value)
    first = lax.axis_index("core") == 0
    return jnp.concatenate([jnp.where(first, value, other), jnp.where(first, other, value)], axis=0)


def pair_sum(value, mask):
    return value + lax.ppermute(value, "y", [(i, i ^ mask) for i in range(4)])


def product(a, b, dims):
    return lax.dot_general(a, b, (dims, ((), ())), precision=HIGH, preferred_element_type=jnp.float32)


def local(gradient, momentum, basis):
    replicas = lax.axis_size("replica")
    rank_local = basis.shape[1]
    buffer = momentum[0] + gradient[0].astype(jnp.float32)

    lines = to_everyone(basis.T, "y")
    other = swapped(lines)
    first = lax.axis_index("core") == 0
    both = jnp.stack([jnp.where(first, lines, other), jnp.where(first, other, lines)], axis=1)
    basis_t = both.reshape(RANK, basis.shape[0])

    part = product(buffer, basis_t, ((1,), (1,)))
    own = scattered_sum(scattered_sum(part, "tensor"), "replica") / replicas
    left = stacked(stacked(own, "replica"), "tensor")

    gram = core_scattered(product(left, left, ((0,), (0,))))
    gram = core_joined(pair_sum(pair_sum(gram, 1), 3))
    inverse = jnp.eye(RANK, dtype=jnp.float32)
    for i in range(RANK // LEAF):
        gram, inverse = factor_part(gram, inverse, i, i + 1)

    raw = product(left, buffer, ((0,), (0,)))
    own = scattered_sum(core_scattered(raw), "y")
    size = own.shape[1] // replicas
    pieces = own.reshape(own.shape[0], replicas, size).swapaxes(0, 1)
    piece = lax.all_to_all(pieces, "replica", 0, 0, tiled=True).sum(axis=0) / replicas
    pieces = to_everyone(piece, "replica")
    own = pieces.swapaxes(0, 1).reshape(own.shape)
    raw = core_joined(stacked(own, "y"))

    right = product(inverse, raw, ((1,), (0,)))
    ortho = product(left, inverse, ((1,), (1,)))
    squares = to_everyone(jnp.sum(right * right, axis=1)[None], "tensor").sum(axis=0)[0]
    norms = jnp.sqrt(squares + 1e-12)
    lowrank = product(ortho, right, ((1,), (0,)))
    momentum_new = (buffer - 0.05 * lowrank)[None]
    scale = (M_ROWS * NCOLS / RANK) ** 0.5
    update = (scale * product(ortho / norms[None], right, ((1,), (0,)))).astype(jnp.bfloat16)
    offset = (lax.axis_index("y") * 2 + lax.axis_index("core")) * rank_local
    mine = lax.dynamic_slice_in_dim(right, offset, rank_local, 0)
    basis_new = (mine / lax.dynamic_slice_in_dim(norms, offset, rank_local, 0)[:, None]).T
    return (update, momentum_new, basis_new)


def solution(mesh):
    finer = Mesh(
        mesh.devices.reshape(4, 2, mesh.shape["tensor"], mesh.shape["replica"]),
        ("y", "core", "tensor", "replica"),
    )
    fsdp = ("y", "core")
    placed = (P("replica", fsdp, "tensor"), P("replica", fsdp, "tensor"), P("tensor", fsdp))
    return jax.shard_map(
        local,
        mesh=finer,
        in_specs=placed,
        out_specs=(P(fsdp, "tensor"), P("replica", fsdp, "tensor"), P("tensor", fsdp)),
        check_vma=False,
    )
```

```python
import functools
import jax, jax.numpy as jnp
from jax import lax
from jax.experimental import pallas as pl
from jax.experimental.pallas import tpu as pltpu
from jax.sharding import Mesh
from jax.sharding import PartitionSpec as P

M_ROWS = 4096
NCOLS = 8192
HIGH = lax.Precision.HIGHEST
RANK = 256
LEAF = 64

def inverted(value):
    near = pl.reciprocal(value, approx=True)
    near = near * (2.0 - value * near)
    return near * (2.0 - value * near)


def leaf_inverse(block):
    side = block.shape[0]
    lane = lax.broadcasted_iota(jnp.int32, (side, side), 1)
    line = lax.broadcasted_iota(jnp.int32, (side, side), 0)
    both = jnp.concatenate([block, jnp.where(lane == line, 1.0, 0.0)], axis=1)
    tiles = [both[at : at + 8] for at in range(0, side, 8)]
    tile = (8, 2 * side)
    sub = lax.broadcasted_iota(jnp.int32, tile, 0)
    for own, rows in enumerate(tiles):
        base = 8 * own
        pivots = [
            [jnp.broadcast_to(rows[i : i + 1, base + j : base + j + 1], tile) for j in range(i + 1)]
            for i in range(8)
        ]
        columns = [
            [jnp.broadcast_to(t[:, base + j : base + j + 1], tile) for j in range(8)]
            for t in tiles[own + 1 :]
        ]
        done = [jnp.broadcast_to(rows[i : i + 1], tile) for i in range(8)]
        lower, inverses = {}, []
        for j in range(8):
            inverse = inverted(pivots[j][j])
            inverses.append(inverse)
            for i in range(j + 1, 8):
                lower[i, j] = pivots[i][j] * inverse
            for i in range(j + 1, 8):
                for m in range(j + 1, i + 1):
                    pivots[i][m] = pivots[i][m] - lower[i, j] * pivots[m][j]
                done[i] = done[i] - lower[i, j] * done[j]
        if own + 1 < len(tiles):
            solved = [None] * 8
            for i in reversed(range(8)):
                solved[i] = done[i] * inverses[i]
                for m in range(i + 1, 8):
                    solved[i] = solved[i] - lower[m, i] * solved[m]
            for g, column in enumerate(columns, own + 1):
                total = column[7] * solved[7]
                for j in reversed(range(7)):
                    total = total + column[j] * solved[j]
                tiles[g] = tiles[g] - total
        final = done[0] * lax.rsqrt(pivots[0][0])
        for i in range(1, 8):
            final = jnp.where(sub == i, done[i] * lax.rsqrt(pivots[i][i]), final)
        tiles[own] = final
    return jnp.concatenate([t[:, side:] for t in tiles], axis=0)


def factor_kernel(first, last, gram_ref, inv_ref, gram_out, inv_out):
    gram_out[...] = gram_ref[...]
    inv_out[...] = inv_ref[...]
    for i in range(first, last):
        lo, hi = i * LEAF, (i + 1) * LEAF
        leaf = leaf_inverse(gram_out[lo:hi, lo:hi])
        rows_g = jnp.dot(leaf, gram_out[lo:hi, :], precision=HIGH, preferred_element_type=jnp.float32)
        rows_i = jnp.dot(leaf, inv_out[lo:hi, :], precision=HIGH, preferred_element_type=jnp.float32)
        inv_out[lo:hi, :] = rows_i
        if hi < RANK:
            cols = rows_g[:, hi:] if hi % 128 == 0 else rows_g[:, hi - 64:]
            tall = cols.T
            if hi % 128: tall = tall[64:]
            gram_out[hi:, :] = gram_out[hi:, :] - jnp.dot(tall, rows_g, precision=HIGH, preferred_element_type=jnp.float32)
            inv_out[hi:, :] = inv_out[hi:, :] - jnp.dot(tall, rows_i, precision=HIGH, preferred_element_type=jnp.float32)

def factor_part(gram, inv, first, last):
    shape = jax.ShapeDtypeStruct((RANK, RANK), jnp.float32)
    return pl.pallas_call(
        functools.partial(factor_kernel, first, last),
        out_shape=(shape, shape),
        compiler_params=pltpu.CompilerParams(vmem_limit_bytes=16 << 20),
        cost_estimate=pl.CostEstimate(flops=0, bytes_accessed=(last-first)*15_000_000, transcendentals=0),
    )(gram, inv)

def to_everyone(value, axis):
    size = lax.axis_size(axis)
    return lax.all_to_all(
        jnp.broadcast_to(value[None], (size, *value.shape)), axis, 0, 0, tiled=True
    )


def stacked(value, axis):
    blocks = to_everyone(value, axis)
    return blocks.reshape(blocks.shape[0] * blocks.shape[1], *blocks.shape[2:])


def parted(value, axis):
    size = lax.axis_size(axis)
    blocks = value.reshape(size, value.shape[0] // size, *value.shape[1:])
    return lax.all_to_all(blocks, axis, 0, 0, tiled=True)


def scattered_sum(value, axis):
    return parted(value, axis).sum(axis=0)


def together(*values):
    return lax.optimization_barrier(values)


def swapped(value):
    return lax.ppermute(value, "core", [(0, 1), (1, 0)])


def core_scattered(value):
    half = value.shape[0] // 2
    core = lax.axis_index("core")
    sent = lax.dynamic_slice_in_dim(value, (1 - core) * half, half, 0)
    kept = lax.dynamic_slice_in_dim(value, core * half, half, 0)
    return kept + swapped(sent)


def core_joined(value):
    other = swapped(value)
    first = lax.axis_index("core") == 0
    return jnp.concatenate([jnp.where(first, value, other), jnp.where(first, other, value)], axis=0)


def pair_sum(value, mask, axis="y"):
    return value + lax.ppermute(value, axis, [(i, i ^ mask) for i in range(4)])


def product(a, b, dims, precision=HIGH):
    return lax.dot_general(a, b, (dims, ((), ())), precision=precision, preferred_element_type=jnp.float32)

def split(value):
    high = value.astype(jnp.bfloat16)
    return high, (value - high.astype(jnp.float32)).astype(jnp.bfloat16)


def three_dots(a, b):
    (a_high, a_low), (b_high, b_low) = a, b

    def dot(one, two):
        return jnp.dot(one, two, preferred_element_type=jnp.float32)

    return dot(a_high, b_high) + (dot(a_high, b_low) + dot(a_low, b_high))


WIDE = 256
IN_VMEM = pl.BlockSpec(memory_space=pltpu.VMEM)
IN_SMEM = pl.BlockSpec(memory_space=pltpu.SMEM)
ANYWHERE = pl.BlockSpec(memory_space=pl.ANY)


def block_of(ref, index):
    return ref.at[:, pl.ds(pl.multiple_of(index * WIDE, WIDE), WIDE)]


def call(kernel, flops, moved, **rest):
    return pl.pallas_call(
        kernel,
        compiler_params=pltpu.CompilerParams(vmem_limit_bytes=24 << 20),
        cost_estimate=pl.CostEstimate(flops=flops, bytes_accessed=moved, transcendentals=0),
        **rest,
    )


def right_kernel(half_ref, left_ref, buffer_ref, out_ref):
    count = out_ref.shape[0]
    left = split(left_ref[...].T)
    for i in range(count):
        block = block_of(buffer_ref, half_ref[0] * count + i)[...]
        out_ref[i] = three_dots(left, split(block))


def right_half(half, left, buffer):
    rows, columns = buffer.shape
    return call(
        right_kernel,
        3 * rows * RANK * columns,
        4 * rows * columns,
        in_specs=[IN_SMEM, IN_VMEM, IN_VMEM],
        out_specs=IN_VMEM,
        out_shape=jax.ShapeDtypeStruct((columns // WIDE // 2, RANK, WIDE), jnp.float32),
    )(half, left, buffer)


def own_kernel(inverse_ref, raw_ref, wide_ref, squares_ref):
    right = jnp.dot(inverse_ref[...], raw_ref[...], precision=HIGH, preferred_element_type=jnp.float32)
    for i in range(wide_ref.shape[0]):
        wide_ref[i] = right
    squares_ref[...] = lax.dot_general(
        jnp.ones((8, WIDE), jnp.float32),
        right * right,
        (((1,), (1,)), ((), ())),
        precision=HIGH,
        preferred_element_type=jnp.float32,
    )


def own_right(inverse, raw, copies):
    return call(
        own_kernel,
        RANK**3,
        RANK * RANK * 32,
        in_specs=[IN_VMEM, IN_VMEM],
        out_specs=(IN_VMEM, IN_VMEM),
        out_shape=(
            jax.ShapeDtypeStruct((copies, RANK, WIDE), jnp.float32),
            jax.ShapeDtypeStruct((8, RANK), jnp.float32),
        ),
    )(inverse, raw)


def change_block(ortho, right, buffer_ref, index, slot_ref, out_ref, sem):
    slot_ref[...] = block_of(buffer_ref, index)[...] + three_dots(ortho, right)
    copy = pltpu.make_async_copy(slot_ref, block_of(out_ref, index), sem)
    copy.start()
    return copy


def first_kernel(half_ref, ortho_ref, right_ref, buffer_ref, out_ref, slots, sems):
    count = right_ref.shape[0]
    ortho = split(ortho_ref[...] * -0.05)
    copies = []
    for i in range(count):
        index = half_ref[0] * count + i
        right = split(right_ref[i])
        copies.append(change_block(ortho, right, buffer_ref, index, slots.at[i], out_ref, sems.at[i]))
    for copy in copies:
        copy.wait()


def first_half(half, ortho, right, buffer):
    rows, columns = buffer.shape
    count = right.shape[0]
    return call(
        first_kernel,
        3 * rows * RANK * columns,
        4 * rows * columns,
        in_specs=[IN_SMEM, IN_VMEM, IN_VMEM, IN_VMEM],
        out_specs=ANYWHERE,
        out_shape=jax.ShapeDtypeStruct((rows, columns), jnp.float32),
        scratch_shapes=[pltpu.VMEM((count, rows, WIDE), jnp.float32), pltpu.SemaphoreType.DMA((count,))],
    )(half, ortho, right, buffer)


def last_kernel(
    place_ref, ortho_ref, mine_ref, other_ref, buffer_ref, squares_ref, filled_ref,
    out_ref, update_ref, lines_ref, column_ref, slots, small, sems, small_sems,
):
    core, offset = place_ref[0], pl.multiple_of(place_ref[1], 32)
    count = mine_ref.shape[0]
    norms = jnp.sqrt(squares_ref[...] + 1e-12)
    column_ref[...] = jnp.concatenate([norms] * 16, axis=0).T
    own_norms = column_ref[pl.ds(offset, 32), :][:, :1]
    ortho = split(ortho_ref[...] * -0.05)
    scaled = split(ortho_ref[...] * ((M_ROWS * NCOLS / RANK) ** 0.5 / norms[:1]))
    copies = []
    for i in range(count):
        index = (1 - core) * count + i
        right = split(other_ref[i])
        copies.append(change_block(ortho, right, buffer_ref, index, slots.at[i], out_ref, sems.at[i]))
    for half, (source, start) in enumerate(((other_ref, (1 - core) * count), (mine_ref, core * count))):
        for i in range(count):
            at = half * count + i
            small[at] = three_dots(scaled, split(source[i])).astype(jnp.bfloat16)
            copy = pltpu.make_async_copy(small.at[at], block_of(update_ref, start + i), small_sems.at[at])
            copy.start()
            copies.append(copy)
            lines = source[i, pl.ds(offset, 32), :] / own_norms
            lines_ref[:, pl.ds(pl.multiple_of((start + i) * WIDE, WIDE), WIDE)] = lines
    for copy in copies:
        copy.wait()


def last_half(place, ortho, mine, other, buffer, squares, filled):
    rows, columns = buffer.shape
    count = mine.shape[0]
    return call(
        last_kernel,
        9 * rows * RANK * columns,
        8 * rows * columns,
        in_specs=[IN_SMEM] + [IN_VMEM] * 5 + [ANYWHERE],
        out_specs=(ANYWHERE, ANYWHERE, IN_VMEM),
        out_shape=(
            jax.ShapeDtypeStruct((rows, columns), jnp.float32),
            jax.ShapeDtypeStruct((rows, columns), jnp.bfloat16),
            jax.ShapeDtypeStruct((32, columns), jnp.float32),
        ),
        scratch_shapes=[
            pltpu.VMEM((RANK, 128), jnp.float32),
            pltpu.VMEM((count, rows, WIDE), jnp.float32),
            pltpu.VMEM((2 * count, rows, WIDE), jnp.bfloat16),
            pltpu.SemaphoreType.DMA((count,)),
            pltpu.SemaphoreType.DMA((2 * count,)),
        ],
        input_output_aliases={6: 0},
    )(place, ortho, mine, other, buffer, squares, filled)


def local(gradient, momentum, basis):
    replicas = lax.axis_size("replica")
    rank_local = basis.shape[1]
    core = lax.axis_index("core")
    first = core == 0
    mine, theirs = jnp.full((1,), core, jnp.int32), jnp.full((1,), 1 - core, jnp.int32)

    wide = jnp.broadcast_to(basis.T[None], (4, rank_local, basis.shape[0]))
    wide, momentum, gradient = together(wide, momentum, gradient)
    lines = lax.all_to_all(wide, "y", 0, 0, tiled=True)
    buffer = momentum[0] + gradient[0].astype(jnp.float32)
    lines, buffer = together(lines, buffer)
    other = swapped(lines)
    both = jnp.stack([jnp.where(first, lines, other), jnp.where(first, other, lines)], axis=1)
    basis_t = both.reshape(RANK, basis.shape[0])

    part = product(buffer, basis_t, ((1,), (1,)), lax.Precision.HIGH)
    own = scattered_sum(scattered_sum(part, "tensor"), "replica") / replicas
    quarter = stacked(own, "replica")
    wide = jnp.broadcast_to(quarter[None], (4, *quarter.shape))
    wide, quarter = together(wide, quarter)
    left = lax.all_to_all(wide, "tensor", 0, 0, tiled=True).reshape(-1, RANK)
    gram = pair_sum(core_scattered(product(quarter, quarter, ((0,), (0,)))), 1)
    left, gram = together(left, gram)
    sent = right_half(theirs, left, buffer)
    gram = pair_sum(gram, 3)
    sent, left = together(sent, left)
    arrived = swapped(sent)
    kept = right_half(mine, left, buffer)
    arrived, kept, gram = together(arrived, kept, gram)
    blocks = lax.all_to_all(arrived + kept, "y", 0, 0, tiled=True)
    gram = core_joined(pair_sum(pair_sum(gram, 1, "tensor"), 3, "tensor"))
    blocks, gram = together(blocks, gram)
    own = blocks.sum(axis=0)
    own, gram = together(own, gram)
    pieces = parted(own, "replica")
    inverse = jnp.eye(RANK, dtype=jnp.float32)
    gram, inverse, pieces = together(*factor_part(gram, inverse, 0, 2), pieces)
    piece = pieces.sum(axis=0) / replicas
    wide = jnp.broadcast_to(piece[None], (replicas, *piece.shape))
    gram, wide = together(gram, wide)
    pieces = lax.all_to_all(wide, "replica", 0, 0, tiled=True)
    gram, inverse, pieces = together(*factor_part(gram, inverse, 2, 4), pieces)
    wide, squares = own_right(inverse, pieces.reshape(RANK, WIDE), 4)
    squares, wide, inverse, left = together(squares, wide, inverse, left)
    right_mine = lax.all_to_all(wide, "y", 0, 0, tiled=True)
    ortho = product(left, inverse, ((1,), (1,)))
    squares = pair_sum(pair_sum(squares, 1, "tensor"), 3, "tensor")
    squares = pair_sum(pair_sum(squares, 1), 3)
    right_mine, ortho, squares = together(right_mine, ortho, squares)
    right_other = swapped(right_mine)
    squares = squares + swapped(squares)

    momentum_new = first_half(mine, ortho, right_mine, buffer)
    momentum_new, right_other, squares = together(momentum_new, right_other, squares)
    place = jnp.stack([core, (lax.axis_index("y") * 2 + core) * rank_local]).astype(jnp.int32)
    momentum_new, update, lines = last_half(place, ortho, right_mine, right_other, buffer, squares, momentum_new)
    return (update, momentum_new[None], lines.T)


def solution(mesh):
    finer = Mesh(
        mesh.devices.reshape(4, 2, mesh.shape["tensor"], mesh.shape["replica"]),
        ("y", "core", "tensor", "replica"),
    )
    fsdp = ("y", "core")
    placed = (P("replica", fsdp, "tensor"), P("replica", fsdp, "tensor"), P("tensor", fsdp))
    return jax.shard_map(
        local,
        mesh=finer,
        in_specs=placed,
        out_specs=(P(fsdp, "tensor"), P("replica", fsdp, "tensor"), P("tensor", fsdp)),
        check_vma=False,
    )
```

```python
import functools
import jax, jax.numpy as jnp
from jax import lax
from jax.experimental import pallas as pl
from jax.experimental.pallas import tpu as pltpu
from jax.sharding import Mesh
from jax.sharding import PartitionSpec as P

M_ROWS = 4096
NCOLS = 8192
HIGH = lax.Precision.HIGHEST
RANK = 256
LEAF = 64

def inverted(value):
    near = pl.reciprocal(value, approx=True)
    near = near * (2.0 - value * near)
    return near * (2.0 - value * near)


def leaf_inverse(block):
    side = block.shape[0]
    lane = lax.broadcasted_iota(jnp.int32, (side, side), 1)
    line = lax.broadcasted_iota(jnp.int32, (side, side), 0)
    both = jnp.concatenate([block, jnp.where(lane == line, 1.0, 0.0)], axis=1)
    tiles = [both[at : at + 8] for at in range(0, side, 8)]
    tile = (8, 2 * side)
    sub = lax.broadcasted_iota(jnp.int32, tile, 0)
    for own, rows in enumerate(tiles):
        base = 8 * own
        pivots = [
            [jnp.broadcast_to(rows[i : i + 1, base + j : base + j + 1], tile) for j in range(i + 1)]
            for i in range(8)
        ]
        columns = [
            [jnp.broadcast_to(t[:, base + j : base + j + 1], tile) for j in range(8)]
            for t in tiles[own + 1 :]
        ]
        done = [jnp.broadcast_to(rows[i : i + 1], tile) for i in range(8)]
        lower, inverses = {}, []
        for j in range(8):
            inverse = inverted(pivots[j][j])
            inverses.append(inverse)
            for i in range(j + 1, 8):
                lower[i, j] = pivots[i][j] * inverse
            for i in range(j + 1, 8):
                for m in range(j + 1, i + 1):
                    pivots[i][m] = pivots[i][m] - lower[i, j] * pivots[m][j]
                done[i] = done[i] - lower[i, j] * done[j]
        if own + 1 < len(tiles):
            solved = [None] * 8
            for i in reversed(range(8)):
                solved[i] = done[i] * inverses[i]
                for m in range(i + 1, 8):
                    solved[i] = solved[i] - lower[m, i] * solved[m]
            for g, column in enumerate(columns, own + 1):
                total = column[7] * solved[7]
                for j in reversed(range(7)):
                    total = total + column[j] * solved[j]
                tiles[g] = tiles[g] - total
        final = done[0] * lax.rsqrt(pivots[0][0])
        for i in range(1, 8):
            final = jnp.where(sub == i, done[i] * lax.rsqrt(pivots[i][i]), final)
        tiles[own] = final
    return jnp.concatenate([t[:, side:] for t in tiles], axis=0)


def factor_kernel(first, last, gram_ref, inv_ref, gram_out, inv_out):
    gram_out[...] = gram_ref[...]
    inv_out[...] = inv_ref[...]
    for i in range(first, last):
        lo, hi = i * LEAF, (i + 1) * LEAF
        leaf = leaf_inverse(gram_out[lo:hi, lo:hi])
        rows_g = jnp.dot(leaf, gram_out[lo:hi, :], precision=HIGH, preferred_element_type=jnp.float32)
        rows_i = jnp.dot(leaf, inv_out[lo:hi, :], precision=HIGH, preferred_element_type=jnp.float32)
        inv_out[lo:hi, :] = rows_i
        if hi < RANK:
            cols = rows_g[:, hi:] if hi % 128 == 0 else rows_g[:, hi - 64:]
            tall = cols.T
            if hi % 128: tall = tall[64:]
            gram_out[hi:, :] = gram_out[hi:, :] - jnp.dot(tall, rows_g, precision=HIGH, preferred_element_type=jnp.float32)
            inv_out[hi:, :] = inv_out[hi:, :] - jnp.dot(tall, rows_i, precision=HIGH, preferred_element_type=jnp.float32)

def factor_part(gram, inv, first, last):
    shape = jax.ShapeDtypeStruct((RANK, RANK), jnp.float32)
    return pl.pallas_call(
        functools.partial(factor_kernel, first, last),
        out_shape=(shape, shape),
        compiler_params=pltpu.CompilerParams(vmem_limit_bytes=16 << 20),
        cost_estimate=pl.CostEstimate(flops=0, bytes_accessed=(last - first) * 10_000, transcendentals=0),
    )(gram, inv)

def to_everyone(value, axis):
    size = lax.axis_size(axis)
    return lax.all_to_all(
        jnp.broadcast_to(value[None], (size, *value.shape)), axis, 0, 0, tiled=True
    )


def stacked(value, axis):
    blocks = to_everyone(value, axis)
    return blocks.reshape(blocks.shape[0] * blocks.shape[1], *blocks.shape[2:])


def parted(value, axis):
    size = lax.axis_size(axis)
    blocks = value.reshape(size, value.shape[0] // size, *value.shape[1:])
    return lax.all_to_all(blocks, axis, 0, 0, tiled=True)


def scattered_sum(value, axis):
    return parted(value, axis).sum(axis=0)


def together(*values):
    return lax.optimization_barrier(values)


def swapped(value):
    return lax.ppermute(value, "core", [(0, 1), (1, 0)])


def core_scattered(value):
    half = value.shape[0] // 2
    core = lax.axis_index("core")
    sent = lax.dynamic_slice_in_dim(value, (1 - core) * half, half, 0)
    kept = lax.dynamic_slice_in_dim(value, core * half, half, 0)
    return kept + swapped(sent)


def core_joined(value):
    other = swapped(value)
    first = lax.axis_index("core") == 0
    return jnp.concatenate([jnp.where(first, value, other), jnp.where(first, other, value)], axis=0)


def pair_sum(value, mask, axis="y"):
    return value + lax.ppermute(value, axis, [(i, i ^ mask) for i in range(4)])


def product(a, b, dims, precision=HIGH):
    return lax.dot_general(a, b, (dims, ((), ())), precision=precision, preferred_element_type=jnp.float32)

def split(value):
    high = value.astype(jnp.bfloat16)
    return high, (value - high.astype(jnp.float32)).astype(jnp.bfloat16)


def three_dots(a, b):
    (a_high, a_low), (b_high, b_low) = a, b

    def dot(one, two):
        return jnp.dot(one, two, preferred_element_type=jnp.float32)

    return dot(a_high, b_high) + (dot(a_high, b_low) + dot(a_low, b_high))


WIDE = 256
IN_VMEM = pl.BlockSpec(memory_space=pltpu.VMEM)
IN_SMEM = pl.BlockSpec(memory_space=pltpu.SMEM)
ANYWHERE = pl.BlockSpec(memory_space=pl.ANY)
IN_HBM = pl.BlockSpec(memory_space=pltpu.HBM)


def block_of(ref, index):
    return ref.at[:, pl.ds(pl.multiple_of(index * WIDE, WIDE), WIDE)]


def call(kernel, flops, moved, **rest):
    return pl.pallas_call(
        kernel,
        compiler_params=pltpu.CompilerParams(vmem_limit_bytes=24 << 20),
        cost_estimate=pl.CostEstimate(flops=flops, bytes_accessed=moved, transcendentals=0),
        **rest,
    )


PARTS = 4


def rows_of(ref, i):
    rows = ref.shape[0] // PARTS
    return ref.at[pl.ds(i * rows, rows), :]


def copied(source, target, sems):
    copies = []
    for i in range(PARTS):
        copy = pltpu.make_async_copy(rows_of(source, i), rows_of(target, i), sems.at[i])
        copy.start()
        copies.append(copy)
    return copies


def added_kernel(momentum_ref, gradient_ref, near_ref, far_ref, low_ref, sems, low_sems, out_sems):
    copies = copied(momentum_ref.at[0], near_ref, sems)
    low_copies = copied(gradient_ref.at[0], low_ref, low_sems)
    out_copies = []
    for i in range(PARTS):
        copies[i].wait()
        low_copies[i].wait()
        rows_of(near_ref, i)[...] = rows_of(near_ref, i)[...] + rows_of(low_ref, i)[...].astype(jnp.float32)
        copy = pltpu.make_async_copy(rows_of(near_ref, i), rows_of(far_ref, i), out_sems.at[i])
        copy.start()
        out_copies.append(copy)
    for copy in out_copies:
        copy.wait()


def added(momentum, gradient):
    _, rows, columns = momentum.shape
    shape = jax.ShapeDtypeStruct((rows, columns), jnp.float32)
    return call(
        added_kernel,
        rows * columns,
        14 * rows * columns,
        in_specs=[IN_HBM, IN_HBM],
        out_specs=(IN_VMEM, IN_HBM),
        out_shape=(shape, shape),
        scratch_shapes=[pltpu.VMEM((rows, columns), jnp.bfloat16)] + [pltpu.SemaphoreType.DMA((PARTS,))] * 3,
    )(momentum, gradient)


def staged_kernel(far_ref, near_ref, sems):
    for copy in copied(far_ref, near_ref, sems):
        copy.wait()


def staged(far):
    return call(
        staged_kernel,
        0,
        8 * far.shape[0] * far.shape[1],
        in_specs=[IN_HBM],
        out_specs=IN_VMEM,
        out_shape=jax.ShapeDtypeStruct(far.shape, jnp.float32),
        scratch_shapes=[pltpu.SemaphoreType.DMA((PARTS,))],
    )(far)


def right_kernel(half_ref, left_ref, buffer_ref, out_ref):
    count = out_ref.shape[0]
    left = split(left_ref[...].T)
    for i in range(count):
        block = block_of(buffer_ref, half_ref[0] * count + i)[...]
        out_ref[i] = three_dots(left, split(block))


def right_half(half, left, buffer):
    rows, columns = buffer.shape
    return call(
        right_kernel,
        3 * rows * RANK * columns,
        4 * rows * columns,
        in_specs=[IN_SMEM, IN_VMEM, IN_VMEM],
        out_specs=IN_VMEM,
        out_shape=jax.ShapeDtypeStruct((columns // WIDE // 2, RANK, WIDE), jnp.float32),
    )(half, left, buffer)


def finished_kernel(inverse_ref, raw_ref, right_ref, squares_ref):
    inverse = split(inverse_ref[...])
    total = jnp.zeros((RANK, WIDE), jnp.float32)
    for i in range(raw_ref.shape[0]):
        right = three_dots(inverse, split(raw_ref[i]))
        right_ref[i] = right
        total = total + right * right
    squares_ref[...] = lax.dot_general(
        jnp.ones((8, WIDE), jnp.float32),
        total,
        (((1,), (1,)), ((), ())),
        precision=HIGH,
        preferred_element_type=jnp.float32,
    )


def finished(inverse, raw):
    return call(
        finished_kernel,
        RANK**3 * 24,
        RANK * RANK * 32,
        in_specs=[IN_VMEM, IN_VMEM],
        out_specs=(IN_VMEM, IN_VMEM),
        out_shape=(
            jax.ShapeDtypeStruct(raw.shape, jnp.float32),
            jax.ShapeDtypeStruct((8, RANK), jnp.float32),
        ),
    )(inverse, raw)


def change_block(ortho, right, buffer_ref, index, slot_ref, out_ref, sem):
    slot_ref[...] = block_of(buffer_ref, index)[...] + three_dots(ortho, right)
    copy = pltpu.make_async_copy(slot_ref, block_of(out_ref, index), sem)
    copy.start()
    return copy


def first_kernel(half_ref, ortho_ref, right_ref, buffer_ref, out_ref, slots, sems):
    count = right_ref.shape[0]
    ortho = split(ortho_ref[...] * -0.05)
    copies = []
    for i in range(count):
        index = half_ref[0] * count + i
        right = split(right_ref[i])
        copies.append(change_block(ortho, right, buffer_ref, index, slots.at[i], out_ref, sems.at[i]))
    for copy in copies:
        copy.wait()


def first_half(half, ortho, right, buffer):
    rows, columns = buffer.shape
    count = right.shape[0]
    return call(
        first_kernel,
        3 * rows * RANK * columns,
        4 * rows * columns,
        in_specs=[IN_SMEM, IN_VMEM, IN_VMEM, IN_VMEM],
        out_specs=ANYWHERE,
        out_shape=jax.ShapeDtypeStruct((rows, columns), jnp.float32),
        scratch_shapes=[pltpu.VMEM((count, rows, WIDE), jnp.float32), pltpu.SemaphoreType.DMA((count,))],
    )(half, ortho, right, buffer)


def last_kernel(
    place_ref, ortho_ref, mine_ref, other_ref, buffer_ref, squares_ref, filled_ref,
    out_ref, update_ref, lines_ref, column_ref, slots, small, sems, small_sems,
):
    core, offset = place_ref[0], pl.multiple_of(place_ref[1], 32)
    count = mine_ref.shape[0]
    norms = jnp.sqrt(squares_ref[...] + 1e-12)
    column_ref[...] = jnp.concatenate([norms] * 16, axis=0).T
    own_norms = column_ref[pl.ds(offset, 32), :][:, :1]
    ortho = split(ortho_ref[...] * -0.05)
    scaled = split(ortho_ref[...] * ((M_ROWS * NCOLS / RANK) ** 0.5 / norms[:1]))
    copies = []
    for i in range(count):
        index = (1 - core) * count + i
        right = split(other_ref[i])
        copies.append(change_block(ortho, right, buffer_ref, index, slots.at[i], out_ref, sems.at[i]))
    for half, (source, start) in enumerate(((other_ref, (1 - core) * count), (mine_ref, core * count))):
        for i in range(count):
            at = half * count + i
            small[at] = three_dots(scaled, split(source[i])).astype(jnp.bfloat16)
            copy = pltpu.make_async_copy(small.at[at], block_of(update_ref, start + i), small_sems.at[at])
            copy.start()
            copies.append(copy)
            lines = source[i, pl.ds(offset, 32), :] / own_norms
            lines_ref[:, pl.ds(pl.multiple_of((start + i) * WIDE, WIDE), WIDE)] = lines
    for copy in copies:
        copy.wait()


def last_half(place, ortho, mine, other, buffer, squares, filled):
    rows, columns = buffer.shape
    count = mine.shape[0]
    return call(
        last_kernel,
        9 * rows * RANK * columns,
        8 * rows * columns,
        in_specs=[IN_SMEM] + [IN_VMEM] * 5 + [ANYWHERE],
        out_specs=(ANYWHERE, ANYWHERE, IN_VMEM),
        out_shape=(
            jax.ShapeDtypeStruct((rows, columns), jnp.float32),
            jax.ShapeDtypeStruct((rows, columns), jnp.bfloat16),
            jax.ShapeDtypeStruct((32, columns), jnp.float32),
        ),
        scratch_shapes=[
            pltpu.VMEM((RANK, 128), jnp.float32),
            pltpu.VMEM((count, rows, WIDE), jnp.float32),
            pltpu.VMEM((2 * count, rows, WIDE), jnp.bfloat16),
            pltpu.SemaphoreType.DMA((count,)),
            pltpu.SemaphoreType.DMA((2 * count,)),
        ],
        input_output_aliases={6: 0},
    )(place, ortho, mine, other, buffer, squares, filled)


def ordered(pieces, position):
    for bit in (1, 2):
        odd = (position & bit) != 0
        pieces = [jnp.where(odd, pieces[j ^ bit], pieces[j]) for j in range(4)]
    return pieces


def turned(value, axis, mask):
    return lax.ppermute(value, axis, [(i, i ^ mask) for i in range(4)])


def product_kernel(a_ref, b_ref, out_ref):
    out_ref[...] = lax.dot_general(
        a_ref[...], b_ref[...], (((1,), (1,)), ((), ())), precision=HIGH, preferred_element_type=jnp.float32
    )


def lines_product(a, b):
    return call(
        product_kernel,
        0,
        14_000_000,
        in_specs=[IN_VMEM, IN_VMEM],
        out_specs=IN_VMEM,
        out_shape=jax.ShapeDtypeStruct((a.shape[0], b.shape[0]), jnp.float32),
    )(a, b)


def whole_sum(value, axis):
    near, across, away = (turned(value, axis, mask) for mask in (1, 2, 3))
    return (value + near) + (across + away)


def whole_sum(value, axis):
    near, across, away = (turned(value, axis, mask) for mask in (1, 2, 3))
    return (value + near) + (across + away)


def local(gradient, momentum, basis):
    replicas = lax.axis_size("replica")
    rank_local = basis.shape[1]
    core, y = lax.axis_index("core"), lax.axis_index("y")
    first = core == 0
    mine, theirs = jnp.full((1,), core, jnp.int32), jnp.full((1,), 1 - core, jnp.int32)
    place = jnp.stack([core, (y * 2 + core) * rank_local]).astype(jnp.int32)

    lines = basis.T
    lines, momentum, gradient = together(lines, momentum, gradient)
    across, near, away = (turned(lines, "y", mask) for mask in (2, 1, 3))
    buffer, far = added(momentum, gradient)
    there = [swapped(lines)]
    near, away, buffer = together(near, away, buffer)
    there += [swapped(near), swapped(across), swapped(away)]
    here = [lines, near, across, away]
    blocks = []
    for ours, others in ((here, there), (there, here)):
        pieces = [jnp.where(first, one, two) for one, two in zip(ours, others)]
        blocks.append(jnp.stack(ordered(pieces, y)))
    basis_t = jnp.stack(blocks, axis=1).reshape(RANK, basis.shape[0])

    part = product(buffer, basis_t, ((1,), (1,)), lax.Precision.HIGH)
    own = scattered_sum(scattered_sum(part, "tensor"), "replica") / replicas
    quarter = stacked(own, "replica")
    quarter, far = together(quarter, far)
    left = [quarter] + [turned(quarter, "tensor", mask) for mask in (1, 2, 3)]
    buffer = staged(far)
    *left, buffer = together(*left, buffer)
    left = jnp.concatenate(ordered(left, lax.axis_index("tensor")), axis=0)
    sent = right_half(theirs, left, buffer)
    sent, left = together(sent, left)
    arrived = swapped(sent)
    gram = product(left, left, ((0,), (0,)))
    kept = right_half(mine, left, buffer)
    arrived, kept, gram = together(arrived, kept, gram)
    blocks = lax.all_to_all(arrived + kept, "y", 0, 0, tiled=True)
    gram = core_scattered(gram)
    blocks, gram = together(blocks, gram)
    own = blocks.sum(axis=0)
    own, gram = together(own, gram)
    pieces = parted(own, "replica")
    gram = whole_sum(gram, "y")
    gram, pieces = together(gram, pieces)
    piece = pieces.sum(axis=0) / replicas
    wide = jnp.broadcast_to(piece[None], (replicas, *piece.shape))
    gram, wide = together(gram, wide)
    pieces = lax.all_to_all(wide, "replica", 0, 0, tiled=True)
    inverse = jnp.eye(RANK, dtype=jnp.float32)
    gram, inverse, pieces = together(*factor_part(core_joined(gram), inverse, 0, 1), pieces)
    wide = jnp.broadcast_to(pieces.reshape(1, RANK, WIDE), (4, RANK, WIDE))
    gram, wide = together(gram, wide)
    raw = lax.all_to_all(wide, "y", 0, 0, tiled=True)
    gram, inverse = factor_part(gram, inverse, 1, 4)
    ortho = lines_product(left, inverse)
    ortho, inverse, raw = together(ortho, inverse, raw)
    right_mine, squares = finished(inverse, raw)
    right_other = swapped(right_mine)
    squares = whole_sum(squares, "tensor")
    momentum_new = first_half(mine, ortho, right_mine, far)
    momentum_new, squares, right_other = together(momentum_new, squares, right_other)
    squares = squares + swapped(squares)
    momentum_new, update, lines = last_half(place, ortho, right_mine, right_other, far, squares, momentum_new)
    return (update, momentum_new[None], lines.T)


def solution(mesh):
    finer = Mesh(
        mesh.devices.reshape(4, 2, mesh.shape["tensor"], mesh.shape["replica"]),
        ("y", "core", "tensor", "replica"),
    )
    fsdp = ("y", "core")
    placed = (P("replica", fsdp, "tensor"), P("replica", fsdp, "tensor"), P("tensor", fsdp))
    return jax.shard_map(
        local,
        mesh=finer,
        in_specs=placed,
        out_specs=(P(fsdp, "tensor"), P("replica", fsdp, "tensor"), P("tensor", fsdp)),
        check_vma=False,
    )
```

```python
import functools
import jax, jax.numpy as jnp
from jax import lax
from jax.experimental import pallas as pl
from jax.experimental.pallas import tpu as pltpu
from jax.sharding import Mesh
from jax.sharding import PartitionSpec as P

M_ROWS = 4096
NCOLS = 8192
HIGH = lax.Precision.HIGHEST
RANK = 256
LEAF = 64

def inverted(value):
    near = pl.reciprocal(value, approx=True)
    near = near * (2.0 - value * near)
    return near * (2.0 - value * near)


def leaf_inverse(block):
    side = block.shape[0]
    lane = lax.broadcasted_iota(jnp.int32, (side, side), 1)
    line = lax.broadcasted_iota(jnp.int32, (side, side), 0)
    both = jnp.concatenate([block, jnp.where(lane == line, 1.0, 0.0)], axis=1)
    tiles = [both[at : at + 8] for at in range(0, side, 8)]
    tile = (8, 2 * side)
    sub = lax.broadcasted_iota(jnp.int32, tile, 0)
    for own, rows in enumerate(tiles):
        base = 8 * own
        pivots = [
            [jnp.broadcast_to(rows[i : i + 1, base + j : base + j + 1], tile) for j in range(i + 1)]
            for i in range(8)
        ]
        columns = [
            [jnp.broadcast_to(t[:, base + j : base + j + 1], tile) for j in range(8)]
            for t in tiles[own + 1 :]
        ]
        done = [jnp.broadcast_to(rows[i : i + 1], tile) for i in range(8)]
        lower, inverses = {}, []
        for j in range(8):
            inverse = inverted(pivots[j][j])
            inverses.append(inverse)
            for i in range(j + 1, 8):
                lower[i, j] = pivots[i][j] * inverse
            for i in range(j + 1, 8):
                for m in range(j + 1, i + 1):
                    pivots[i][m] = pivots[i][m] - lower[i, j] * pivots[m][j]
                done[i] = done[i] - lower[i, j] * done[j]
        if own + 1 < len(tiles):
            solved = [None] * 8
            for i in reversed(range(8)):
                solved[i] = done[i] * inverses[i]
                for m in range(i + 1, 8):
                    solved[i] = solved[i] - lower[m, i] * solved[m]
            for g, column in enumerate(columns, own + 1):
                total = column[7] * solved[7]
                for j in reversed(range(7)):
                    total = total + column[j] * solved[j]
                tiles[g] = tiles[g] - total
        final = done[0] * lax.rsqrt(pivots[0][0])
        for i in range(1, 8):
            final = jnp.where(sub == i, done[i] * lax.rsqrt(pivots[i][i]), final)
        tiles[own] = final
    return jnp.concatenate([t[:, side:] for t in tiles], axis=0)


def factor_kernel(first, last, gram_ref, inv_ref, gram_out, inv_out):
    gram_out[...] = gram_ref[...]
    inv_out[...] = inv_ref[...]
    for i in range(first, last):
        lo, hi = i * LEAF, (i + 1) * LEAF
        leaf = leaf_inverse(gram_out[lo:hi, lo:hi])
        rows_g = jnp.dot(leaf, gram_out[lo:hi, :], precision=HIGH, preferred_element_type=jnp.float32)
        rows_i = jnp.dot(leaf, inv_out[lo:hi, :], precision=HIGH, preferred_element_type=jnp.float32)
        inv_out[lo:hi, :] = rows_i
        if hi < RANK:
            cols = rows_g[:, hi:] if hi % 128 == 0 else rows_g[:, hi - 64:]
            tall = cols.T
            if hi % 128: tall = tall[64:]
            gram_out[hi:, :] = gram_out[hi:, :] - jnp.dot(tall, rows_g, precision=HIGH, preferred_element_type=jnp.float32)
            inv_out[hi:, :] = inv_out[hi:, :] - jnp.dot(tall, rows_i, precision=HIGH, preferred_element_type=jnp.float32)

def factor_part(gram, inv, first, last):
    shape = jax.ShapeDtypeStruct((RANK, RANK), jnp.float32)
    return pl.pallas_call(
        functools.partial(factor_kernel, first, last),
        out_shape=(shape, shape),
        compiler_params=pltpu.CompilerParams(vmem_limit_bytes=16 << 20),
        cost_estimate=pl.CostEstimate(flops=0, bytes_accessed=(last - first) * 10_000, transcendentals=0),
    )(gram, inv)

def to_everyone(value, axis):
    size = lax.axis_size(axis)
    return lax.all_to_all(
        jnp.broadcast_to(value[None], (size, *value.shape)), axis, 0, 0, tiled=True
    )


def stacked(value, axis):
    blocks = to_everyone(value, axis)
    return blocks.reshape(blocks.shape[0] * blocks.shape[1], *blocks.shape[2:])


def parted(value, axis):
    size = lax.axis_size(axis)
    blocks = value.reshape(size, value.shape[0] // size, *value.shape[1:])
    return lax.all_to_all(blocks, axis, 0, 0, tiled=True)


def scattered_sum(value, axis):
    return parted(value, axis).sum(axis=0)


def together(*values):
    return lax.optimization_barrier(values)


def swapped(value):
    return lax.ppermute(value, "core", [(0, 1), (1, 0)])


def core_scattered(value):
    half = value.shape[0] // 2
    core = lax.axis_index("core")
    sent = lax.dynamic_slice_in_dim(value, (1 - core) * half, half, 0)
    kept = lax.dynamic_slice_in_dim(value, core * half, half, 0)
    return kept + swapped(sent)


def core_joined(value):
    other = swapped(value)
    first = lax.axis_index("core") == 0
    return jnp.concatenate([jnp.where(first, value, other), jnp.where(first, other, value)], axis=0)


def pair_sum(value, mask, axis="y"):
    return value + lax.ppermute(value, axis, [(i, i ^ mask) for i in range(4)])


def product(a, b, dims, precision=HIGH):
    return lax.dot_general(a, b, (dims, ((), ())), precision=precision, preferred_element_type=jnp.float32)

def split(value):
    high = value.astype(jnp.bfloat16)
    return high, (value - high.astype(jnp.float32)).astype(jnp.bfloat16)


def three_dots(a, b):
    (a_high, a_low), (b_high, b_low) = a, b

    def dot(one, two):
        return jnp.dot(one, two, preferred_element_type=jnp.float32)

    return dot(a_high, b_high) + (dot(a_high, b_low) + dot(a_low, b_high))


WIDE = 256
IN_VMEM = pl.BlockSpec(memory_space=pltpu.VMEM)
IN_SMEM = pl.BlockSpec(memory_space=pltpu.SMEM)
ANYWHERE = pl.BlockSpec(memory_space=pl.ANY)
IN_HBM = pl.BlockSpec(memory_space=pltpu.HBM)


def block_of(ref, index):
    return ref.at[:, pl.ds(pl.multiple_of(index * WIDE, WIDE), WIDE)]


def call(kernel, flops, moved, **rest):
    return pl.pallas_call(
        kernel,
        compiler_params=pltpu.CompilerParams(vmem_limit_bytes=24 << 20),
        cost_estimate=pl.CostEstimate(flops=flops, bytes_accessed=moved, transcendentals=0),
        **rest,
    )


PARTS = 4


def rows_of(ref, i):
    rows = ref.shape[0] // PARTS
    return ref.at[pl.ds(i * rows, rows), :]


def copied(source, target, sems):
    copies = []
    for i in range(PARTS):
        copy = pltpu.make_async_copy(rows_of(source, i), rows_of(target, i), sems.at[i])
        copy.start()
        copies.append(copy)
    return copies


def added_kernel(momentum_ref, gradient_ref, near_ref, far_ref, low_ref, sems, low_sems, out_sems):
    copies = copied(momentum_ref.at[0], near_ref, sems)
    low_copies = copied(gradient_ref.at[0], low_ref, low_sems)
    out_copies = []
    for i in range(PARTS):
        copies[i].wait()
        low_copies[i].wait()
        rows_of(near_ref, i)[...] = rows_of(near_ref, i)[...] + rows_of(low_ref, i)[...].astype(jnp.float32)
        copy = pltpu.make_async_copy(rows_of(near_ref, i), rows_of(far_ref, i), out_sems.at[i])
        copy.start()
        out_copies.append(copy)
    for copy in out_copies:
        copy.wait()


def added(momentum, gradient):
    _, rows, columns = momentum.shape
    shape = jax.ShapeDtypeStruct((rows, columns), jnp.float32)
    return call(
        added_kernel,
        rows * columns,
        14 * rows * columns,
        in_specs=[IN_HBM, IN_HBM],
        out_specs=(IN_VMEM, IN_HBM),
        out_shape=(shape, shape),
        scratch_shapes=[pltpu.VMEM((rows, columns), jnp.bfloat16)] + [pltpu.SemaphoreType.DMA((PARTS,))] * 3,
    )(momentum, gradient)


def staged_kernel(far_ref, near_ref, sems):
    for copy in copied(far_ref, near_ref, sems):
        copy.wait()


def staged(far):
    return call(
        staged_kernel,
        0,
        8 * far.shape[0] * far.shape[1],
        in_specs=[IN_HBM],
        out_specs=IN_VMEM,
        out_shape=jax.ShapeDtypeStruct(far.shape, jnp.float32),
        scratch_shapes=[pltpu.SemaphoreType.DMA((PARTS,))],
    )(far)


def right_kernel(place_ref, left_ref, buffer_ref, sent_ref, kept_ref):
    count = kept_ref.shape[0]
    left = split(left_ref[...].T)
    for core, out_ref in ((1 - place_ref[0], sent_ref), (place_ref[0], kept_ref)):
        for turn in range(count):
            block = block_of(buffer_ref, core * count + (place_ref[1] ^ turn))[...]
            out_ref[turn] = three_dots(left, split(block))


def right_parts(place, left, buffer):
    rows, columns = buffer.shape
    shape = jax.ShapeDtypeStruct((columns // WIDE // 2, RANK, WIDE), jnp.float32)
    return call(
        right_kernel,
        6 * rows * RANK * columns,
        8 * rows * columns,
        in_specs=[IN_SMEM, IN_VMEM, IN_VMEM],
        out_specs=(IN_VMEM, IN_VMEM),
        out_shape=(shape, shape),
    )(place, left, buffer)


def finished_kernel(inverse_ref, raw_ref, right_ref, squares_ref):
    inverse = split(inverse_ref[...])
    total = jnp.zeros((RANK, WIDE), jnp.float32)
    for i in range(raw_ref.shape[0]):
        right = three_dots(inverse, split(raw_ref[i]))
        right_ref[i] = right
        total = total + right * right
    squares_ref[...] = lax.dot_general(
        jnp.ones((8, WIDE), jnp.float32),
        total,
        (((1,), (1,)), ((), ())),
        precision=HIGH,
        preferred_element_type=jnp.float32,
    )


def finished(inverse, raw):
    return call(
        finished_kernel,
        RANK**3 * 24,
        RANK * RANK * 32,
        in_specs=[IN_VMEM, IN_VMEM],
        out_specs=(IN_VMEM, IN_VMEM),
        out_shape=(
            jax.ShapeDtypeStruct(raw.shape, jnp.float32),
            jax.ShapeDtypeStruct((8, RANK), jnp.float32),
        ),
    )(inverse, raw)


def change_block(ortho, right, buffer_ref, index, slot_ref, out_ref, sem):
    slot_ref[...] = block_of(buffer_ref, index)[...] + three_dots(ortho, right)
    copy = pltpu.make_async_copy(slot_ref, block_of(out_ref, index), sem)
    copy.start()
    return copy


def first_kernel(half_ref, ortho_ref, right_ref, buffer_ref, out_ref, slots, sems):
    count = right_ref.shape[0]
    ortho = split(ortho_ref[...] * -0.05)
    copies = []
    for i in range(count):
        index = half_ref[0] * count + i
        right = split(right_ref[i])
        copies.append(change_block(ortho, right, buffer_ref, index, slots.at[i], out_ref, sems.at[i]))
    for copy in copies:
        copy.wait()


def first_half(half, ortho, right, buffer):
    rows, columns = buffer.shape
    count = right.shape[0]
    return call(
        first_kernel,
        3 * rows * RANK * columns,
        4 * rows * columns,
        in_specs=[IN_SMEM, IN_VMEM, IN_VMEM, IN_VMEM],
        out_specs=ANYWHERE,
        out_shape=jax.ShapeDtypeStruct((rows, columns), jnp.float32),
        scratch_shapes=[pltpu.VMEM((count, rows, WIDE), jnp.float32), pltpu.SemaphoreType.DMA((count,))],
    )(half, ortho, right, buffer)


def last_kernel(
    place_ref, ortho_ref, mine_ref, other_ref, buffer_ref, squares_ref, filled_ref,
    out_ref, update_ref, lines_ref, column_ref, slots, small, sems, small_sems,
):
    core, offset = place_ref[0], pl.multiple_of(place_ref[1], 32)
    count = mine_ref.shape[0]
    norms = jnp.sqrt(squares_ref[...] + 1e-12)
    column_ref[...] = jnp.concatenate([norms] * 16, axis=0).T
    own_norms = column_ref[pl.ds(offset, 32), :][:, :1]
    ortho = split(ortho_ref[...] * -0.05)
    scaled = split(ortho_ref[...] * ((M_ROWS * NCOLS / RANK) ** 0.5 / norms[:1]))
    copies = []
    for i in range(count):
        index = (1 - core) * count + i
        right = split(other_ref[i])
        copies.append(change_block(ortho, right, buffer_ref, index, slots.at[i], out_ref, sems.at[i]))
    for half, (source, start) in enumerate(((other_ref, (1 - core) * count), (mine_ref, core * count))):
        for i in range(count):
            at = half * count + i
            small[at] = three_dots(scaled, split(source[i])).astype(jnp.bfloat16)
            copy = pltpu.make_async_copy(small.at[at], block_of(update_ref, start + i), small_sems.at[at])
            copy.start()
            copies.append(copy)
            lines = source[i, pl.ds(offset, 32), :] / own_norms
            lines_ref[:, pl.ds(pl.multiple_of((start + i) * WIDE, WIDE), WIDE)] = lines
    for copy in copies:
        copy.wait()


def last_half(place, ortho, mine, other, buffer, squares, filled):
    rows, columns = buffer.shape
    count = mine.shape[0]
    return call(
        last_kernel,
        9 * rows * RANK * columns,
        8 * rows * columns,
        in_specs=[IN_SMEM] + [IN_VMEM] * 5 + [ANYWHERE],
        out_specs=(ANYWHERE, ANYWHERE, IN_VMEM),
        out_shape=(
            jax.ShapeDtypeStruct((rows, columns), jnp.float32),
            jax.ShapeDtypeStruct((rows, columns), jnp.bfloat16),
            jax.ShapeDtypeStruct((32, columns), jnp.float32),
        ),
        scratch_shapes=[
            pltpu.VMEM((RANK, 128), jnp.float32),
            pltpu.VMEM((count, rows, WIDE), jnp.float32),
            pltpu.VMEM((2 * count, rows, WIDE), jnp.bfloat16),
            pltpu.SemaphoreType.DMA((count,)),
            pltpu.SemaphoreType.DMA((2 * count,)),
        ],
        input_output_aliases={6: 0},
    )(place, ortho, mine, other, buffer, squares, filled)


def ordered(pieces, position):
    for bit in (1, 2):
        odd = (position & bit) != 0
        pieces = [jnp.where(odd, pieces[j ^ bit], pieces[j]) for j in range(4)]
    return pieces


def turned(value, axis, mask):
    return lax.ppermute(value, axis, [(i, i ^ mask) for i in range(4)])


def product_kernel(a_ref, b_ref, out_ref):
    out_ref[...] = lax.dot_general(
        a_ref[...], b_ref[...], (((1,), (1,)), ((), ())), precision=HIGH, preferred_element_type=jnp.float32
    )


def lines_product(a, b):
    return call(
        product_kernel,
        0,
        14_000_000,
        in_specs=[IN_VMEM, IN_VMEM],
        out_specs=IN_VMEM,
        out_shape=jax.ShapeDtypeStruct((a.shape[0], b.shape[0]), jnp.float32),
    )(a, b)


def owner_sum(blocks, axis):
    position = lax.axis_index(axis)

    def picked(mask):
        return lax.dynamic_index_in_dim(blocks, position ^ mask, 0, keepdims=False)

    across, near, away = (turned(picked(mask), axis, mask) for mask in (2, 1, 3))
    return (picked(0) + near) + (across + away)


def whole_sum(value, axis):
    near, across, away = (turned(value, axis, mask) for mask in (1, 2, 3))
    return (value + near) + (across + away)


def whole_sum(value, axis):
    near, across, away = (turned(value, axis, mask) for mask in (1, 2, 3))
    return (value + near) + (across + away)


def local(gradient, momentum, basis):
    replicas = lax.axis_size("replica")
    rank_local = basis.shape[1]
    core, y = lax.axis_index("core"), lax.axis_index("y")
    first = core == 0
    mine = jnp.full((1,), core, jnp.int32)
    place = jnp.stack([core, (y * 2 + core) * rank_local]).astype(jnp.int32)

    lines = basis.T
    lines, momentum, gradient = together(lines, momentum, gradient)
    across, near, away = (turned(lines, "y", mask) for mask in (2, 1, 3))
    buffer, far = added(momentum, gradient)
    there = [swapped(lines)]
    near, away, buffer = together(near, away, buffer)
    there += [swapped(near), swapped(across), swapped(away)]
    here = [lines, near, across, away]
    blocks = []
    for ours, others in ((here, there), (there, here)):
        pieces = [jnp.where(first, one, two) for one, two in zip(ours, others)]
        blocks.append(jnp.stack(ordered(pieces, y)))
    basis_t = jnp.stack(blocks, axis=1).reshape(RANK, basis.shape[0])

    part = product(buffer, basis_t, ((1,), (1,)), lax.Precision.HIGH)
    part = owner_sum(part.reshape(4, -1, RANK), "tensor")
    own = scattered_sum(part, "replica") / replicas
    quarter = stacked(own, "replica")
    quarter, far = together(quarter, far)
    left = [quarter] + [turned(quarter, "tensor", mask) for mask in (1, 2, 3)]
    buffer = staged(far)
    *left, buffer = together(*left, buffer)
    left = jnp.concatenate(ordered(left, lax.axis_index("tensor")), axis=0)
    sent, kept = right_parts(jnp.stack([core, y]).astype(jnp.int32), left, buffer)
    sent, kept, left = together(sent, kept, left)
    arrived = swapped(sent)
    gram = product(left, left, ((0,), (0,)))
    arrived, gram = together(arrived, gram)
    own, *others = [arrived[turn] + kept[turn] for turn in range(4)]
    across, near, away = (turned(others[mask - 1], "y", mask) for mask in (2, 1, 3))
    own = (own + near) + (across + away)
    gram = core_scattered(gram)
    own, gram = together(own, gram)
    pieces = parted(own, "replica")
    gram = whole_sum(gram, "y")
    gram, pieces = together(gram, pieces)
    piece = pieces.sum(axis=0) / replicas
    wide = jnp.broadcast_to(piece[None], (replicas, *piece.shape))
    gram, wide = together(gram, wide)
    pieces = lax.all_to_all(wide, "replica", 0, 0, tiled=True)
    inverse = jnp.eye(RANK, dtype=jnp.float32)
    gram, inverse, pieces = together(*factor_part(core_joined(gram), inverse, 0, 1), pieces)
    wide = jnp.broadcast_to(pieces.reshape(1, RANK, WIDE), (4, RANK, WIDE))
    gram, wide = together(gram, wide)
    raw = lax.all_to_all(wide, "y", 0, 0, tiled=True)
    gram, inverse = factor_part(gram, inverse, 1, 4)
    ortho = lines_product(left, inverse)
    ortho, inverse, raw = together(ortho, inverse, raw)
    right_mine, squares = finished(inverse, raw)
    right_other = swapped(right_mine)
    squares = whole_sum(squares, "tensor")
    momentum_new = first_half(mine, ortho, right_mine, far)
    momentum_new, squares, right_other = together(momentum_new, squares, right_other)
    squares = squares + swapped(squares)
    momentum_new, update, lines = last_half(place, ortho, right_mine, right_other, far, squares, momentum_new)
    return (update, momentum_new[None], lines.T)


def solution(mesh):
    finer = Mesh(
        mesh.devices.reshape(4, 2, mesh.shape["tensor"], mesh.shape["replica"]),
        ("y", "core", "tensor", "replica"),
    )
    fsdp = ("y", "core")
    placed = (P("replica", fsdp, "tensor"), P("replica", fsdp, "tensor"), P("tensor", fsdp))
    return jax.shard_map(
        local,
        mesh=finer,
        in_specs=placed,
        out_specs=(P(fsdp, "tensor"), P("replica", fsdp, "tensor"), P("tensor", fsdp)),
        check_vma=False,
    )
```

```python
import functools
import jax, jax.numpy as jnp
from jax import lax
from jax.experimental import pallas as pl
from jax.experimental.pallas import tpu as pltpu
from jax.sharding import Mesh
from jax.sharding import PartitionSpec as P

M_ROWS = 4096
NCOLS = 8192
HIGH = lax.Precision.HIGHEST
RANK = 256
LEAF = 64

def inverted(value):
    near = pl.reciprocal(value, approx=True)
    return near * (2.0 - value * near)


def leaf_inverse(block):
    side = block.shape[0]
    lane = lax.broadcasted_iota(jnp.int32, (side, side), 1)
    line = lax.broadcasted_iota(jnp.int32, (side, side), 0)
    both = jnp.concatenate([block, jnp.where(lane == line, 1.0, 0.0)], axis=1)
    tiles = [both[at : at + 8] for at in range(0, side, 8)]
    tile = (8, 2 * side)
    sub = lax.broadcasted_iota(jnp.int32, tile, 0)
    for own, rows in enumerate(tiles):
        base = 8 * own
        pivots = [
            [jnp.broadcast_to(rows[i : i + 1, base + j : base + j + 1], tile) for j in range(i + 1)]
            for i in range(8)
        ]
        columns = [
            [jnp.broadcast_to(t[:, base + j : base + j + 1], tile) for j in range(8)]
            for t in tiles[own + 1 :]
        ]
        done = [jnp.broadcast_to(rows[i : i + 1], tile) for i in range(8)]
        lower, inverses = {}, []
        for j in range(8):
            inverse = inverted(pivots[j][j])
            inverses.append(inverse)
            for i in range(j + 1, 8):
                lower[i, j] = pivots[i][j] * inverse
            for i in range(j + 1, 8):
                for m in range(j + 1, i + 1):
                    pivots[i][m] = pivots[i][m] - lower[i, j] * pivots[m][j]
                done[i] = done[i] - lower[i, j] * done[j]
        if own + 1 < len(tiles):
            solved = [None] * 8
            for i in reversed(range(8)):
                solved[i] = done[i] * inverses[i]
                for m in range(i + 1, 8):
                    solved[i] = solved[i] - lower[m, i] * solved[m]
            for g, column in enumerate(columns, own + 1):
                total = column[7] * solved[7]
                for j in reversed(range(7)):
                    total = total + column[j] * solved[j]
                tiles[g] = tiles[g] - total
        final = done[0] * lax.rsqrt(pivots[0][0])
        for i in range(1, 8):
            final = jnp.where(sub == i, done[i] * lax.rsqrt(pivots[i][i]), final)
        tiles[own] = final
    return jnp.concatenate([t[:, side:] for t in tiles], axis=0)


def factor_kernel(first, last, gram_ref, inv_ref, gram_out, inv_out):
    gram_out[...] = gram_ref[...]
    inv_out[...] = inv_ref[...]
    for i in range(first, last):
        lo, hi = i * LEAF, (i + 1) * LEAF
        leaf = leaf_inverse(gram_out[lo:hi, lo:hi])
        rows_g = jnp.dot(leaf, gram_out[lo:hi, :], precision=HIGH, preferred_element_type=jnp.float32)
        rows_i = jnp.dot(leaf, inv_out[lo:hi, :], precision=HIGH, preferred_element_type=jnp.float32)
        inv_out[lo:hi, :] = rows_i
        if hi < RANK:
            cols = rows_g[:, hi:] if hi % 128 == 0 else rows_g[:, hi - 64:]
            tall = cols.T
            if hi % 128: tall = tall[64:]
            gram_out[hi:, :] = gram_out[hi:, :] - jnp.dot(tall, rows_g, precision=HIGH, preferred_element_type=jnp.float32)
            inv_out[hi:, :] = inv_out[hi:, :] - jnp.dot(tall, rows_i, precision=HIGH, preferred_element_type=jnp.float32)

def factor_part(gram, inv, first, last):
    shape = jax.ShapeDtypeStruct((RANK, RANK), jnp.float32)
    return pl.pallas_call(
        functools.partial(factor_kernel, first, last),
        out_shape=(shape, shape),
        compiler_params=pltpu.CompilerParams(vmem_limit_bytes=16 << 20),
        cost_estimate=pl.CostEstimate(flops=0, bytes_accessed=(last - first) * 10_000, transcendentals=0),
    )(gram, inv)

def to_everyone(value, axis):
    size = lax.axis_size(axis)
    return lax.all_to_all(
        jnp.broadcast_to(value[None], (size, *value.shape)), axis, 0, 0, tiled=True
    )


def stacked(value, axis):
    blocks = to_everyone(value, axis)
    return blocks.reshape(blocks.shape[0] * blocks.shape[1], *blocks.shape[2:])


def parted(value, axis):
    size = lax.axis_size(axis)
    blocks = value.reshape(size, value.shape[0] // size, *value.shape[1:])
    return lax.all_to_all(blocks, axis, 0, 0, tiled=True)


def scattered_sum(value, axis):
    return parted(value, axis).sum(axis=0)


def together(*values):
    return lax.optimization_barrier(values)


def swapped(value):
    return lax.ppermute(value, "core", [(0, 1), (1, 0)])


def core_scattered(value):
    half = value.shape[0] // 2
    core = lax.axis_index("core")
    sent = lax.dynamic_slice_in_dim(value, (1 - core) * half, half, 0)
    kept = lax.dynamic_slice_in_dim(value, core * half, half, 0)
    return kept + swapped(sent)


def core_joined(value):
    other = swapped(value)
    first = lax.axis_index("core") == 0
    return jnp.concatenate([jnp.where(first, value, other), jnp.where(first, other, value)], axis=0)


def pair_sum(value, mask, axis="y"):
    return value + lax.ppermute(value, axis, [(i, i ^ mask) for i in range(4)])


def product(a, b, dims, precision=HIGH):
    return lax.dot_general(a, b, (dims, ((), ())), precision=precision, preferred_element_type=jnp.float32)

def split(value):
    high = value.astype(jnp.bfloat16)
    return high, (value - high.astype(jnp.float32)).astype(jnp.bfloat16)


def three_dots(a, b):
    (a_high, a_low), (b_high, b_low) = a, b

    def dot(one, two):
        return jnp.dot(one, two, preferred_element_type=jnp.float32)

    return dot(a_high, b_high) + (dot(a_high, b_low) + dot(a_low, b_high))


WIDE = 256
IN_VMEM = pl.BlockSpec(memory_space=pltpu.VMEM)
IN_SMEM = pl.BlockSpec(memory_space=pltpu.SMEM)
ANYWHERE = pl.BlockSpec(memory_space=pl.ANY)
IN_HBM = pl.BlockSpec(memory_space=pltpu.HBM)


def block_of(ref, index):
    return ref.at[:, pl.ds(pl.multiple_of(index * WIDE, WIDE), WIDE)]


def call(kernel, flops, moved, **rest):
    return pl.pallas_call(
        kernel,
        compiler_params=pltpu.CompilerParams(vmem_limit_bytes=24 << 20),
        cost_estimate=pl.CostEstimate(flops=flops, bytes_accessed=moved, transcendentals=0),
        **rest,
    )


PARTS = 4


def rows_of(ref, i):
    rows = ref.shape[0] // PARTS
    return ref.at[pl.ds(i * rows, rows), :]


def copied(source, target, sems):
    copies = []
    for i in range(PARTS):
        copy = pltpu.make_async_copy(rows_of(source, i), rows_of(target, i), sems.at[i])
        copy.start()
        copies.append(copy)
    return copies


def added_kernel(momentum_ref, gradient_ref, near_ref, far_ref, low_ref, sems, low_sems, out_sems):
    copies = copied(momentum_ref.at[0], near_ref, sems)
    low_copies = copied(gradient_ref.at[0], low_ref, low_sems)
    out_copies = []
    for i in range(PARTS):
        copies[i].wait()
        low_copies[i].wait()
        rows_of(near_ref, i)[...] = rows_of(near_ref, i)[...] + rows_of(low_ref, i)[...].astype(jnp.float32)
        copy = pltpu.make_async_copy(rows_of(near_ref, i), rows_of(far_ref, i), out_sems.at[i])
        copy.start()
        out_copies.append(copy)
    for copy in out_copies:
        copy.wait()


def added(momentum, gradient):
    _, rows, columns = momentum.shape
    shape = jax.ShapeDtypeStruct((rows, columns), jnp.float32)
    return call(
        added_kernel,
        rows * columns,
        14 * rows * columns,
        in_specs=[IN_HBM, IN_HBM],
        out_specs=(IN_VMEM, IN_HBM),
        out_shape=(shape, shape),
        scratch_shapes=[pltpu.VMEM((rows, columns), jnp.bfloat16)] + [pltpu.SemaphoreType.DMA((PARTS,))] * 3,
    )(momentum, gradient)


def staged_kernel(far_ref, near_ref, sems):
    for copy in copied(far_ref, near_ref, sems):
        copy.wait()


def staged(far):
    return call(
        staged_kernel,
        0,
        8 * far.shape[0] * far.shape[1],
        in_specs=[IN_HBM],
        out_specs=IN_VMEM,
        out_shape=jax.ShapeDtypeStruct(far.shape, jnp.float32),
        scratch_shapes=[pltpu.SemaphoreType.DMA((PARTS,))],
    )(far)


def right_kernel(place_ref, left_ref, buffer_ref, sent_ref, kept_ref):
    count = kept_ref.shape[0]
    left = split(left_ref[...].T)
    for core, out_ref in ((1 - place_ref[0], sent_ref), (place_ref[0], kept_ref)):
        for turn in range(count):
            block = block_of(buffer_ref, core * count + (place_ref[1] ^ turn))[...]
            out_ref[turn] = three_dots(left, split(block))


def right_parts(place, left, buffer):
    rows, columns = buffer.shape
    shape = jax.ShapeDtypeStruct((columns // WIDE // 2, RANK, WIDE), jnp.float32)
    return call(
        right_kernel,
        6 * rows * RANK * columns,
        8 * rows * columns,
        in_specs=[IN_SMEM, IN_VMEM, IN_VMEM],
        out_specs=(IN_VMEM, IN_VMEM),
        out_shape=(shape, shape),
    )(place, left, buffer)


def finished_kernel(inverse_ref, raw_ref, right_ref, squares_ref):
    inverse = split(inverse_ref[...])
    total = jnp.zeros((RANK, WIDE), jnp.float32)
    for i in range(raw_ref.shape[0]):
        right = three_dots(inverse, split(raw_ref[i]))
        right_ref[i] = right
        total = total + right * right
    squares_ref[...] = lax.dot_general(
        jnp.ones((8, WIDE), jnp.float32),
        total,
        (((1,), (1,)), ((), ())),
        precision=HIGH,
        preferred_element_type=jnp.float32,
    )


def finished(inverse, raw):
    return call(
        finished_kernel,
        RANK**3 * 24,
        RANK * RANK * 32,
        in_specs=[IN_VMEM, IN_VMEM],
        out_specs=(IN_VMEM, IN_VMEM),
        out_shape=(
            jax.ShapeDtypeStruct(raw.shape, jnp.float32),
            jax.ShapeDtypeStruct((8, RANK), jnp.float32),
        ),
    )(inverse, raw)


def change_block(ortho, right, buffer_ref, index, slot_ref, out_ref, sem):
    change = jnp.dot(ortho, right.astype(jnp.bfloat16), preferred_element_type=jnp.float32)
    slot_ref[...] = block_of(buffer_ref, index)[...] + change
    copy = pltpu.make_async_copy(slot_ref, block_of(out_ref, index), sem)
    copy.start()
    return copy


def first_kernel(half_ref, ortho_ref, right_ref, buffer_ref, out_ref, slots, sems):
    count = right_ref.shape[0]
    ortho = (ortho_ref[...] * -0.05).astype(jnp.bfloat16)
    copies = []
    for i in range(count):
        index = half_ref[0] * count + i
        right = right_ref[i]
        copies.append(change_block(ortho, right, buffer_ref, index, slots.at[i], out_ref, sems.at[i]))
    for copy in copies:
        copy.wait()


def first_half(half, ortho, right, buffer):
    rows, columns = buffer.shape
    count = right.shape[0]
    return call(
        first_kernel,
        3 * rows * RANK * columns,
        4 * rows * columns,
        in_specs=[IN_SMEM, IN_VMEM, IN_VMEM, IN_VMEM],
        out_specs=ANYWHERE,
        out_shape=jax.ShapeDtypeStruct((rows, columns), jnp.float32),
        scratch_shapes=[pltpu.VMEM((count, rows, WIDE), jnp.float32), pltpu.SemaphoreType.DMA((count,))],
    )(half, ortho, right, buffer)


def last_kernel(
    place_ref, ortho_ref, mine_ref, other_ref, buffer_ref, squares_ref, filled_ref,
    out_ref, update_ref, lines_ref, column_ref, slots, small, sems, small_sems,
):
    core, offset = place_ref[0], pl.multiple_of(place_ref[1], 32)
    count = mine_ref.shape[0]
    norms = jnp.sqrt(squares_ref[...] + 1e-12)
    column_ref[...] = jnp.concatenate([norms] * 16, axis=0).T
    own_norms = column_ref[pl.ds(offset, 32), :][:, :1]
    ortho = (ortho_ref[...] * -0.05).astype(jnp.bfloat16)
    scaled = split(ortho_ref[...] * ((M_ROWS * NCOLS / RANK) ** 0.5 / norms[:1]))
    copies = []
    for i in range(count):
        index = (1 - core) * count + i
        right = other_ref[i]
        copies.append(change_block(ortho, right, buffer_ref, index, slots.at[i], out_ref, sems.at[i]))
    for half, (source, start) in enumerate(((other_ref, (1 - core) * count), (mine_ref, core * count))):
        for i in range(count):
            at = half * count + i
            small[at] = three_dots(scaled, split(source[i])).astype(jnp.bfloat16)
            copy = pltpu.make_async_copy(small.at[at], block_of(update_ref, start + i), small_sems.at[at])
            copy.start()
            copies.append(copy)
            lines = source[i, pl.ds(offset, 32), :] / own_norms
            lines_ref[:, pl.ds(pl.multiple_of((start + i) * WIDE, WIDE), WIDE)] = lines
    for copy in copies:
        copy.wait()


def last_half(place, ortho, mine, other, buffer, squares, filled):
    rows, columns = buffer.shape
    count = mine.shape[0]
    return call(
        last_kernel,
        9 * rows * RANK * columns,
        8 * rows * columns,
        in_specs=[IN_SMEM] + [IN_VMEM] * 5 + [ANYWHERE],
        out_specs=(ANYWHERE, ANYWHERE, IN_VMEM),
        out_shape=(
            jax.ShapeDtypeStruct((rows, columns), jnp.float32),
            jax.ShapeDtypeStruct((rows, columns), jnp.bfloat16),
            jax.ShapeDtypeStruct((32, columns), jnp.float32),
        ),
        scratch_shapes=[
            pltpu.VMEM((RANK, 128), jnp.float32),
            pltpu.VMEM((count, rows, WIDE), jnp.float32),
            pltpu.VMEM((2 * count, rows, WIDE), jnp.bfloat16),
            pltpu.SemaphoreType.DMA((count,)),
            pltpu.SemaphoreType.DMA((2 * count,)),
        ],
        input_output_aliases={6: 0},
    )(place, ortho, mine, other, buffer, squares, filled)


def ordered(pieces, position):
    for bit in (1, 2):
        odd = (position & bit) != 0
        pieces = [jnp.where(odd, pieces[j ^ bit], pieces[j]) for j in range(4)]
    return pieces


def turned(value, axis, mask):
    return lax.ppermute(value, axis, [(i, i ^ mask) for i in range(4)])


def product_kernel(a_ref, b_ref, out_ref):
    out_ref[...] = lax.dot_general(
        a_ref[...], b_ref[...], (((1,), (1,)), ((), ())), precision=HIGH, preferred_element_type=jnp.float32
    )


def lines_product(a, b):
    return call(
        product_kernel,
        0,
        14_000_000,
        in_specs=[IN_VMEM, IN_VMEM],
        out_specs=IN_VMEM,
        out_shape=jax.ShapeDtypeStruct((a.shape[0], b.shape[0]), jnp.float32),
    )(a, b)


def owner_sum(blocks, axis):
    position = lax.axis_index(axis)

    def picked(mask):
        return lax.dynamic_index_in_dim(blocks, position ^ mask, 0, keepdims=False)

    across, near, away = (turned(picked(mask), axis, mask) for mask in (2, 1, 3))
    return (picked(0) + near) + (across + away)


def whole_sum(value, axis):
    near, across, away = (turned(value, axis, mask) for mask in (1, 2, 3))
    return (value + near) + (across + away)


def whole_sum(value, axis):
    near, across, away = (turned(value, axis, mask) for mask in (1, 2, 3))
    return (value + near) + (across + away)


def local(gradient, momentum, basis):
    replicas = lax.axis_size("replica")
    rank_local = basis.shape[1]
    core, y = lax.axis_index("core"), lax.axis_index("y")
    first = core == 0
    mine = jnp.full((1,), core, jnp.int32)
    place = jnp.stack([core, (y * 2 + core) * rank_local]).astype(jnp.int32)

    lines = basis.T
    lines, momentum, gradient = together(lines, momentum, gradient)
    across, near, away = (turned(lines, "y", mask) for mask in (2, 1, 3))
    buffer, far = added(momentum, gradient)
    there = [swapped(lines)]
    near, away, buffer = together(near, away, buffer)
    there += [swapped(near), swapped(across), swapped(away)]
    here = [lines, near, across, away]
    blocks = []
    for ours, others in ((here, there), (there, here)):
        pieces = [jnp.where(first, one, two) for one, two in zip(ours, others)]
        blocks.append(jnp.stack(ordered(pieces, y)))
    basis_t = jnp.stack(blocks, axis=1).reshape(RANK, basis.shape[0])

    part = product(buffer, basis_t, ((1,), (1,)), lax.Precision.HIGH)
    part = owner_sum(part.reshape(4, -1, RANK), "tensor")
    own = scattered_sum(part, "replica") / replicas
    quarter = stacked(own, "replica")
    quarter, far = together(quarter, far)
    left = [quarter] + [turned(quarter, "tensor", mask) for mask in (1, 2, 3)]
    buffer = staged(far)
    *left, buffer = together(*left, buffer)
    left = jnp.concatenate(ordered(left, lax.axis_index("tensor")), axis=0)
    sent, kept = right_parts(jnp.stack([core, y]).astype(jnp.int32), left, buffer)
    sent, kept, left = together(sent, kept, left)
    arrived = swapped(sent)
    gram = product(left, left, ((0,), (0,)))
    arrived, gram = together(arrived, gram)
    own, *others = [arrived[turn] + kept[turn] for turn in range(4)]
    across, near, away = (turned(others[mask - 1], "y", mask) for mask in (2, 1, 3))
    own = (own + near) + (across + away)
    gram = core_scattered(gram)
    own, gram = together(own, gram)
    pieces = parted(own, "replica")
    gram = whole_sum(gram, "y")
    gram, pieces = together(gram, pieces)
    piece = pieces.sum(axis=0) / replicas
    wide = jnp.broadcast_to(piece[None], (replicas, *piece.shape))
    gram, wide = together(gram, wide)
    pieces = lax.all_to_all(wide, "replica", 0, 0, tiled=True)
    inverse = jnp.eye(RANK, dtype=jnp.float32)
    gram, inverse, pieces = together(*factor_part(core_joined(gram), inverse, 0, 1), pieces)
    wide = jnp.broadcast_to(pieces.reshape(1, RANK, WIDE), (4, RANK, WIDE))
    gram, wide = together(gram, wide)
    raw = lax.all_to_all(wide, "y", 0, 0, tiled=True)
    gram, inverse = factor_part(gram, inverse, 1, 4)
    ortho = lines_product(left, inverse)
    ortho, inverse, raw = together(ortho, inverse, raw)
    right_mine, squares = finished(inverse, raw)
    right_other = swapped(right_mine)
    squares = whole_sum(squares, "tensor")
    momentum_new = first_half(mine, ortho, right_mine, far)
    momentum_new, squares, right_other = together(momentum_new, squares, right_other)
    squares = squares + swapped(squares)
    momentum_new, update, lines = last_half(place, ortho, right_mine, right_other, far, squares, momentum_new)
    return (update, momentum_new[None], lines.T)


def solution(mesh):
    finer = Mesh(
        mesh.devices.reshape(4, 2, mesh.shape["tensor"], mesh.shape["replica"]),
        ("y", "core", "tensor", "replica"),
    )
    fsdp = ("y", "core")
    placed = (P("replica", fsdp, "tensor"), P("replica", fsdp, "tensor"), P("tensor", fsdp))
    return jax.shard_map(
        local,
        mesh=finer,
        in_specs=placed,
        out_specs=(P(fsdp, "tensor"), P("replica", fsdp, "tensor"), P("tensor", fsdp)),
        check_vma=False,
    )
```

```python
import functools
import jax, jax.numpy as jnp
from jax import lax
from jax.experimental import pallas as pl
from jax.experimental.pallas import tpu as pltpu
from jax.sharding import Mesh
from jax.sharding import PartitionSpec as P

M_ROWS = 4096
NCOLS = 8192
HIGH = lax.Precision.HIGHEST
RANK = 256
LEAF = 64

def inverted(value):
    near = pl.reciprocal(value, approx=True)
    return near * (2.0 - value * near)


def leaf_inverse(block):
    side = block.shape[0]
    lane = lax.broadcasted_iota(jnp.int32, (side, side), 1)
    line = lax.broadcasted_iota(jnp.int32, (side, side), 0)
    both = jnp.concatenate([block, jnp.where(lane == line, 1.0, 0.0)], axis=1)
    tiles = [both[at : at + 8] for at in range(0, side, 8)]
    tile = (8, 2 * side)
    sub = lax.broadcasted_iota(jnp.int32, tile, 0)
    for own, rows in enumerate(tiles):
        base = 8 * own
        pivots = [
            [jnp.broadcast_to(rows[i : i + 1, base + j : base + j + 1], tile) for j in range(i + 1)]
            for i in range(8)
        ]
        columns = [
            [jnp.broadcast_to(t[:, base + j : base + j + 1], tile) for j in range(8)]
            for t in tiles[own + 1 :]
        ]
        done = [jnp.broadcast_to(rows[i : i + 1], tile) for i in range(8)]
        lower, inverses = {}, []
        for j in range(8):
            inverse = inverted(pivots[j][j])
            inverses.append(inverse)
            for i in range(j + 1, 8):
                lower[i, j] = pivots[i][j] * inverse
            for i in range(j + 1, 8):
                for m in range(j + 1, i + 1):
                    pivots[i][m] = pivots[i][m] - lower[i, j] * pivots[m][j]
                done[i] = done[i] - lower[i, j] * done[j]
        if own + 1 < len(tiles):
            solved = [None] * 8
            for i in reversed(range(8)):
                solved[i] = done[i] * inverses[i]
                for m in range(i + 1, 8):
                    solved[i] = solved[i] - lower[m, i] * solved[m]
            for g, column in enumerate(columns, own + 1):
                total = column[7] * solved[7]
                for j in reversed(range(7)):
                    total = total + column[j] * solved[j]
                tiles[g] = tiles[g] - total
        final = done[0] * lax.rsqrt(pivots[0][0])
        for i in range(1, 8):
            final = jnp.where(sub == i, done[i] * lax.rsqrt(pivots[i][i]), final)
        tiles[own] = final
    return jnp.concatenate([t[:, side:] for t in tiles], axis=0)


def factor_kernel(first, last, gram_ref, inv_ref, gram_out, inv_out):
    gram_out[...] = gram_ref[...]
    inv_out[...] = inv_ref[...]
    for i in range(first, last):
        lo, hi = i * LEAF, (i + 1) * LEAF
        leaf = leaf_inverse(gram_out[lo:hi, lo:hi])
        rows_g = jnp.dot(leaf, gram_out[lo:hi, :], precision=HIGH, preferred_element_type=jnp.float32)
        rows_i = jnp.dot(leaf, inv_out[lo:hi, :], precision=HIGH, preferred_element_type=jnp.float32)
        inv_out[lo:hi, :] = rows_i
        if hi < RANK:
            cols = rows_g[:, hi:] if hi % 128 == 0 else rows_g[:, hi - 64:]
            tall = cols.T
            if hi % 128: tall = tall[64:]
            gram_out[hi:, :] = gram_out[hi:, :] - jnp.dot(tall, rows_g, precision=HIGH, preferred_element_type=jnp.float32)
            inv_out[hi:, :] = inv_out[hi:, :] - jnp.dot(tall, rows_i, precision=HIGH, preferred_element_type=jnp.float32)

def factor_part(gram, inv, first, last):
    shape = jax.ShapeDtypeStruct((RANK, RANK), jnp.float32)
    return pl.pallas_call(
        functools.partial(factor_kernel, first, last),
        out_shape=(shape, shape),
        compiler_params=pltpu.CompilerParams(vmem_limit_bytes=16 << 20),
        cost_estimate=pl.CostEstimate(flops=0, bytes_accessed=(last - first) * 10_000, transcendentals=0),
    )(gram, inv)

def to_everyone(value, axis):
    size = lax.axis_size(axis)
    return lax.all_to_all(
        jnp.broadcast_to(value[None], (size, *value.shape)), axis, 0, 0, tiled=True
    )


def stacked(value, axis):
    blocks = to_everyone(value, axis)
    return blocks.reshape(blocks.shape[0] * blocks.shape[1], *blocks.shape[2:])


def parted(value, axis):
    size = lax.axis_size(axis)
    blocks = value.reshape(size, value.shape[0] // size, *value.shape[1:])
    return lax.all_to_all(blocks, axis, 0, 0, tiled=True)


def scattered_sum(value, axis):
    return parted(value, axis).sum(axis=0)


def together(*values):
    return lax.optimization_barrier(values)


def swapped(value):
    return lax.ppermute(value, "core", [(0, 1), (1, 0)])


def core_scattered(value):
    half = value.shape[0] // 2
    core = lax.axis_index("core")
    sent = lax.dynamic_slice_in_dim(value, (1 - core) * half, half, 0)
    kept = lax.dynamic_slice_in_dim(value, core * half, half, 0)
    return kept + swapped(sent)


def core_joined(value):
    other = swapped(value)
    first = lax.axis_index("core") == 0
    return jnp.concatenate([jnp.where(first, value, other), jnp.where(first, other, value)], axis=0)


def pair_sum(value, mask, axis="y"):
    return value + lax.ppermute(value, axis, [(i, i ^ mask) for i in range(4)])


def product(a, b, dims, precision=HIGH):
    return lax.dot_general(a, b, (dims, ((), ())), precision=precision, preferred_element_type=jnp.float32)

def split(value):
    high = value.astype(jnp.bfloat16)
    return high, (value - high.astype(jnp.float32)).astype(jnp.bfloat16)


def three_dots(a, b):
    (a_high, a_low), (b_high, b_low) = a, b

    def dot(one, two):
        return jnp.dot(one, two, preferred_element_type=jnp.float32)

    return dot(a_high, b_high) + (dot(a_high, b_low) + dot(a_low, b_high))


WIDE = 256
IN_VMEM = pl.BlockSpec(memory_space=pltpu.VMEM)
IN_SMEM = pl.BlockSpec(memory_space=pltpu.SMEM)
ANYWHERE = pl.BlockSpec(memory_space=pl.ANY)
IN_HBM = pl.BlockSpec(memory_space=pltpu.HBM)


def block_of(ref, index):
    return ref.at[:, pl.ds(pl.multiple_of(index * WIDE, WIDE), WIDE)]


def call(kernel, flops, moved, **rest):
    return pl.pallas_call(
        kernel,
        compiler_params=pltpu.CompilerParams(vmem_limit_bytes=24 << 20),
        cost_estimate=pl.CostEstimate(flops=flops, bytes_accessed=moved, transcendentals=0),
        **rest,
    )


PARTS = 4


def rows_of(ref, i):
    rows = ref.shape[0] // PARTS
    return ref.at[pl.ds(i * rows, rows), :]


def copied(source, target, sems):
    copies = []
    for i in range(PARTS):
        copy = pltpu.make_async_copy(rows_of(source, i), rows_of(target, i), sems.at[i])
        copy.start()
        copies.append(copy)
    return copies


def added_kernel(momentum_ref, gradient_ref, near_ref, far_ref, low_ref, sems, low_sems, out_sems):
    copies = copied(momentum_ref.at[0], near_ref, sems)
    low_copies = copied(gradient_ref.at[0], low_ref, low_sems)
    out_copies = []
    for i in range(PARTS):
        copies[i].wait()
        low_copies[i].wait()
        rows_of(near_ref, i)[...] = rows_of(near_ref, i)[...] + rows_of(low_ref, i)[...].astype(jnp.float32)
        copy = pltpu.make_async_copy(rows_of(near_ref, i), rows_of(far_ref, i), out_sems.at[i])
        copy.start()
        out_copies.append(copy)
    for copy in out_copies:
        copy.wait()


def added(momentum, gradient):
    _, rows, columns = momentum.shape
    shape = jax.ShapeDtypeStruct((rows, columns), jnp.float32)
    return call(
        added_kernel,
        rows * columns,
        14 * rows * columns,
        in_specs=[IN_HBM, IN_HBM],
        out_specs=(IN_VMEM, IN_HBM),
        out_shape=(shape, shape),
        scratch_shapes=[pltpu.VMEM((rows, columns), jnp.bfloat16)] + [pltpu.SemaphoreType.DMA((PARTS,))] * 3,
    )(momentum, gradient)


def staged_kernel(far_ref, near_ref, sems):
    for copy in copied(far_ref, near_ref, sems):
        copy.wait()


def staged(far):
    return call(
        staged_kernel,
        0,
        8 * far.shape[0] * far.shape[1],
        in_specs=[IN_HBM],
        out_specs=IN_VMEM,
        out_shape=jax.ShapeDtypeStruct(far.shape, jnp.float32),
        scratch_shapes=[pltpu.SemaphoreType.DMA((PARTS,))],
    )(far)


def right_kernel(place_ref, left_ref, buffer_ref, sent_ref, kept_ref):
    count = kept_ref.shape[0]
    left = split(left_ref[...].T)
    for core, out_ref in ((1 - place_ref[0], sent_ref), (place_ref[0], kept_ref)):
        for turn in range(count):
            block = block_of(buffer_ref, core * count + (place_ref[1] ^ turn))[...]
            out_ref[turn] = three_dots(left, split(block))


def right_parts(place, left, buffer):
    rows, columns = buffer.shape
    shape = jax.ShapeDtypeStruct((columns // WIDE // 2, RANK, WIDE), jnp.float32)
    return call(
        right_kernel,
        6 * rows * RANK * columns,
        8 * rows * columns,
        in_specs=[IN_SMEM, IN_VMEM, IN_VMEM],
        out_specs=(IN_VMEM, IN_VMEM),
        out_shape=(shape, shape),
    )(place, left, buffer)


def finished_kernel(inverse_ref, raw_ref, right_ref, squares_ref):
    inverse = split(inverse_ref[...])
    total = jnp.zeros((RANK, WIDE), jnp.float32)
    for i in range(raw_ref.shape[0]):
        right = three_dots(inverse, split(raw_ref[i]))
        right_ref[i] = right
        total = total + right * right
    squares_ref[...] = lax.dot_general(
        jnp.ones((8, WIDE), jnp.float32),
        total,
        (((1,), (1,)), ((), ())),
        precision=HIGH,
        preferred_element_type=jnp.float32,
    )


def finished(inverse, raw):
    return call(
        finished_kernel,
        RANK**3 * 24,
        RANK * RANK * 32,
        in_specs=[IN_VMEM, IN_VMEM],
        out_specs=(IN_VMEM, IN_VMEM),
        out_shape=(
            jax.ShapeDtypeStruct(raw.shape, jnp.float32),
            jax.ShapeDtypeStruct((8, RANK), jnp.float32),
        ),
    )(inverse, raw)


def change_block(ortho, right, buffer_ref, index, slot_ref, out_ref, sem):
    change = jnp.dot(ortho, right.astype(jnp.bfloat16), preferred_element_type=jnp.float32)
    slot_ref[...] = block_of(buffer_ref, index)[...] + change
    copy = pltpu.make_async_copy(slot_ref, block_of(out_ref, index), sem)
    copy.start()
    return copy


def first_kernel(half_ref, ortho_ref, right_ref, buffer_ref, out_ref, slots, sems):
    count = right_ref.shape[0]
    ortho = (ortho_ref[...] * -0.05).astype(jnp.bfloat16)
    copies = []
    for i in range(count):
        index = half_ref[0] * count + i
        right = right_ref[i]
        copies.append(change_block(ortho, right, buffer_ref, index, slots.at[i], out_ref, sems.at[i]))
    for copy in copies:
        copy.wait()


def first_half(half, ortho, right, buffer):
    rows, columns = buffer.shape
    count = right.shape[0]
    return call(
        first_kernel,
        3 * rows * RANK * columns,
        4 * rows * columns,
        in_specs=[IN_SMEM, IN_VMEM, IN_VMEM, IN_VMEM],
        out_specs=ANYWHERE,
        out_shape=jax.ShapeDtypeStruct((rows, columns), jnp.float32),
        scratch_shapes=[pltpu.VMEM((count, rows, WIDE), jnp.float32), pltpu.SemaphoreType.DMA((count,))],
    )(half, ortho, right, buffer)


def last_kernel(
    place_ref, ortho_ref, mine_ref, other_ref, buffer_ref, squares_ref, filled_ref,
    out_ref, update_ref, lines_ref, column_ref, slots, small, sems, small_sems,
):
    core, offset = place_ref[0], pl.multiple_of(place_ref[1], 32)
    count = mine_ref.shape[0]
    norms = jnp.sqrt(squares_ref[...] + 1e-12)
    column_ref[...] = jnp.concatenate([norms] * 16, axis=0).T
    own_norms = column_ref[pl.ds(offset, 32), :][:, :1]
    ortho = (ortho_ref[...] * -0.05).astype(jnp.bfloat16)
    scaled = split(ortho_ref[...] * ((M_ROWS * NCOLS / RANK) ** 0.5 / norms[:1]))
    copies = []
    for i in range(count):
        index = (1 - core) * count + i
        right = other_ref[i]
        copies.append(change_block(ortho, right, buffer_ref, index, slots.at[i], out_ref, sems.at[i]))
    for half, (source, start) in enumerate(((other_ref, (1 - core) * count), (mine_ref, core * count))):
        for i in range(count):
            at = half * count + i
            small[at] = three_dots(scaled, split(source[i])).astype(jnp.bfloat16)
            copy = pltpu.make_async_copy(small.at[at], block_of(update_ref, start + i), small_sems.at[at])
            copy.start()
            copies.append(copy)
            lines = source[i, pl.ds(offset, 32), :] / own_norms
            lines_ref[:, pl.ds(pl.multiple_of((start + i) * WIDE, WIDE), WIDE)] = lines
    for copy in copies:
        copy.wait()


def last_half(place, ortho, mine, other, buffer, squares, filled):
    rows, columns = buffer.shape
    count = mine.shape[0]
    return call(
        last_kernel,
        9 * rows * RANK * columns,
        8 * rows * columns,
        in_specs=[IN_SMEM] + [IN_VMEM] * 5 + [ANYWHERE],
        out_specs=(ANYWHERE, ANYWHERE, IN_VMEM),
        out_shape=(
            jax.ShapeDtypeStruct((rows, columns), jnp.float32),
            jax.ShapeDtypeStruct((rows, columns), jnp.bfloat16),
            jax.ShapeDtypeStruct((32, columns), jnp.float32),
        ),
        scratch_shapes=[
            pltpu.VMEM((RANK, 128), jnp.float32),
            pltpu.VMEM((count, rows, WIDE), jnp.float32),
            pltpu.VMEM((2 * count, rows, WIDE), jnp.bfloat16),
            pltpu.SemaphoreType.DMA((count,)),
            pltpu.SemaphoreType.DMA((2 * count,)),
        ],
        input_output_aliases={6: 0},
    )(place, ortho, mine, other, buffer, squares, filled)


def ordered(pieces, position):
    for bit in (1, 2):
        odd = (position & bit) != 0
        pieces = [jnp.where(odd, pieces[j ^ bit], pieces[j]) for j in range(4)]
    return pieces


def turned(value, axis, mask):
    return lax.ppermute(value, axis, [(i, i ^ mask) for i in range(4)])


def product_kernel(a_ref, b_ref, out_ref):
    out_ref[...] = lax.dot_general(
        a_ref[...], b_ref[...], (((1,), (1,)), ((), ())), precision=HIGH, preferred_element_type=jnp.float32
    )


def lines_product(a, b):
    return call(
        product_kernel,
        0,
        14_000_000,
        in_specs=[IN_VMEM, IN_VMEM],
        out_specs=IN_VMEM,
        out_shape=jax.ShapeDtypeStruct((a.shape[0], b.shape[0]), jnp.float32),
    )(a, b)


def owner_sum(blocks, axis):
    position = lax.axis_index(axis)

    def picked(mask):
        return lax.dynamic_index_in_dim(blocks, position ^ mask, 0, keepdims=False)

    across, near, away = (turned(picked(mask), axis, mask) for mask in (2, 1, 3))
    return (picked(0) + near) + (across + away)


def whole_sum(value, axis):
    near, across, away = (turned(value, axis, mask) for mask in (1, 2, 3))
    return (value + near) + (across + away)


def whole_sum(value, axis):
    near, across, away = (turned(value, axis, mask) for mask in (1, 2, 3))
    return (value + near) + (across + away)


def local(gradient, momentum, basis):
    replicas = lax.axis_size("replica")
    rank_local = basis.shape[1]
    core, y = lax.axis_index("core"), lax.axis_index("y")
    first = core == 0
    mine = jnp.full((1,), core, jnp.int32)
    place = jnp.stack([core, (y * 2 + core) * rank_local]).astype(jnp.int32)

    lines = basis.T
    lines, momentum, gradient = together(lines, momentum, gradient)
    across, near, away = (turned(lines, "y", mask) for mask in (2, 1, 3))
    buffer, far = added(momentum, gradient)
    there = [swapped(lines)]
    near, away, buffer = together(near, away, buffer)
    there += [swapped(near), swapped(across), swapped(away)]
    here = [lines, near, across, away]
    blocks = []
    for ours, others in ((here, there), (there, here)):
        pieces = [jnp.where(first, one, two) for one, two in zip(ours, others)]
        blocks.append(jnp.stack(ordered(pieces, y)))
    basis_t = jnp.stack(blocks, axis=1).reshape(RANK, basis.shape[0])

    part = product(buffer, basis_t, ((1,), (1,)), lax.Precision.HIGH)
    part = owner_sum(part.reshape(4, -1, RANK), "tensor")
    own = scattered_sum(part, "replica") / replicas
    quarter = stacked(own, "replica")
    quarter, far = together(quarter, far)
    left = [quarter] + [turned(quarter, "tensor", mask) for mask in (1, 2, 3)]
    buffer = staged(far)
    *left, buffer = together(*left, buffer)
    left = jnp.concatenate(ordered(left, lax.axis_index("tensor")), axis=0)
    sent, kept = right_parts(jnp.stack([core, y]).astype(jnp.int32), left, buffer)
    sent, kept, left = together(sent, kept, left)
    arrived = swapped(sent)
    gram = product(left, left, ((0,), (0,)))
    arrived, gram = together(arrived, gram)
    own, *others = [arrived[turn] + kept[turn] for turn in range(4)]
    across, near, away = (turned(others[mask - 1], "y", mask) for mask in (2, 1, 3))
    own = (own + near) + (across + away)
    gram = core_scattered(gram)
    own, gram = together(own, gram)
    pieces = parted(own, "replica")
    gram = whole_sum(gram, "y")
    gram, pieces = together(gram, pieces)
    piece = pieces.sum(axis=0) / replicas
    wide = jnp.broadcast_to(piece[None], (replicas, *piece.shape))
    gram, wide = together(gram, wide)
    pieces = lax.all_to_all(wide, "replica", 0, 0, tiled=True)
    inverse = jnp.eye(RANK, dtype=jnp.float32)
    gram, inverse, pieces = together(*factor_part(core_joined(gram), inverse, 0, 2), pieces)
    wide = jnp.broadcast_to(pieces.reshape(1, RANK, WIDE), (4, RANK, WIDE))
    gram, wide = together(gram, wide)
    raw = lax.all_to_all(wide, "y", 0, 0, tiled=True)
    gram, inverse = factor_part(gram, inverse, 2, 4)
    ortho = lines_product(left, inverse)
    ortho, inverse, raw = together(ortho, inverse, raw)
    right_mine, squares = finished(inverse, raw)
    right_other = swapped(right_mine)
    squares = whole_sum(squares, "tensor")
    momentum_new = first_half(mine, ortho, right_mine, far)
    momentum_new, squares, right_other = together(momentum_new, squares, right_other)
    squares = squares + swapped(squares)
    momentum_new, update, lines = last_half(place, ortho, right_mine, right_other, far, squares, momentum_new)
    return (update, momentum_new[None], lines.T)


def solution(mesh):
    finer = Mesh(
        mesh.devices.reshape(4, 2, mesh.shape["tensor"], mesh.shape["replica"]),
        ("y", "core", "tensor", "replica"),
    )
    fsdp = ("y", "core")
    placed = (P("replica", fsdp, "tensor"), P("replica", fsdp, "tensor"), P("tensor", fsdp))
    return jax.shard_map(
        local,
        mesh=finer,
        in_specs=placed,
        out_specs=(P(fsdp, "tensor"), P("replica", fsdp, "tensor"), P("tensor", fsdp)),
        check_vma=False,
    )
```
